32 devices in a mesh: dec: 8 (over y, x, core), ch: 4 (over z).
Axes of the slice: x: 2, y: 2, z: 4, core: 2. Of those that a mesh axis runs over, the one named last changes fastest.
Arguments:
- frame_cotangent: bfloat16 [64, 160, 8192], P('dec', None, 'ch'), may hold values from -5 to 5
- rollout_utterance: int32 [64], P('dec'), may hold values from 0 to 7, as said below
- frame_offset: int32 [64], P('dec'), may hold values from 0 to 32
- utterance_frames: int32 [8], P('dec'), may hold values from 1 to 128, 768 in all
- normed_input: bfloat16 [8, 128, 1024], P('dec', None, 'ch'), may hold values from -6 to 6
- expand_weight: bfloat16 [1024, 2, 1024], P(None, None, 'ch'), may hold values from -0.1875 to 0.1875
- depth_kernel: bfloat16 [9, 1024], P(None, 'ch'), may hold values from -2 to 2
- norm_scale: float32 [1024], P('ch'), may hold values from 0.1 to 1.9
- norm_shift: float32 [1024], P('ch'), may hold values from -3 to 3
- project_weight: bfloat16 [1024, 1024], replicated, may hold values from -0.1875 to 0.1875
- adapter_weight: bfloat16 [1024, 8192], P(None, 'ch'), may hold values from -0.0625 to 0.0625
Outputs:
- grad_stream: bfloat16 [8, 128, 1024], P('dec', None, 'ch')
- grad_normed: bfloat16 [8, 128, 1024], P('dec', None, 'ch')
The draws below stay inside these ranges and needn't reach their ends.
Inputs may be any that keep to these rules, and one draw needn't show every extreme that they name: `rollout_utterance`: each utterance is named by exactly 8 rollouts; utterances k * 1 to (k + 1) - 1 are owned by index k of dec; among the 8 rollouts of one index of dec at most 1 name utterances of one owner, and some owner is named exactly 1 times; the rollouts of index k of dec always name some utterance of the owner (k + 4) mod 8.
All inputs are finite; a program needn't handle non-finite values. No bound on the sum of `utterance_frames` on one device may be relied on, other than what follows from the above.
Results may differ from the reference program's by a relative error of at most 0.03.
Values may be sent and summed in bfloat16 or wider, within the bound.
No kernel may reach another device: no remote copies, remote signals or barrier semaphores. Data moves between devices by JAX's collectives and lax.ppermute only.
A program may use at most 128 MiB of HBM per device.

```python
import math
import jax
import jax.numpy as jnp
import numpy as np
from jax import lax

D = 8192
C = 1024
K = 9
U_DEV = 1
F = 128
PROMPT = 32
SEQ = 160
UTT = 8
R_DEV = 8
ROLLOUTS = 64
ROUTE_CAP = 1
N_DEC = 8


def draw_rollout_utterance(key, part):
    total_slots = N_DEC * ROUTE_CAP
    shuffled_slots = jax.random.permutation(jax.random.fold_in(key, 11), total_slots).astype(jnp.int32)
    far_slot = jnp.argmax((shuffled_slots == N_DEC // 2).astype(jnp.int32)).astype(jnp.int32)
    chosen = jnp.roll(shuffled_slots, -far_slot)[:R_DEV].astype(jnp.int32)
    ranking = jnp.argsort(jnp.argsort(chosen)).astype(jnp.int32)
    offsets = chosen % N_DEC
    within = ranking % U_DEV
    devices = jnp.arange(N_DEC, dtype=jnp.int32)[:, None]
    owners = (devices + offsets[None, :]) % N_DEC
    utts = owners * U_DEV + within[None, :]
    keys = jax.random.split(jax.random.fold_in(key, 23), N_DEC)
    orders = jax.vmap(lambda single: jax.random.permutation(single, R_DEV))(keys)
    shuffled = jnp.take_along_axis(utts, orders.astype(jnp.int32), axis=1)
    return shuffled.reshape(ROLLOUTS).astype(jnp.int32)


def place_ends(values, own_key, least, largest):
    spot = [jax.random.randint(jax.random.fold_in(own_key, axis), (), 0, length) for axis, length in enumerate(values.shape)]
    main_axis = values.shape.index(max(values.shape))
    next_to = spot[:main_axis] + [(spot[main_axis] + 1) % values.shape[main_axis]] + spot[main_axis + 1:]
    return values.at[tuple(spot)].set(least).at[tuple(next_to)].set(largest)


def level_of(key, dims, cuts, low, largest):
    level = 1.0
    for axis_at, shards_of in cuts:
        draws = jax.random.uniform(jax.random.fold_in(jax.random.fold_in(key, 6), axis_at), (shards_of,), jnp.float32, low / len(cuts), largest / len(cuts))
        level = level * jnp.repeat(jnp.exp(draws), dims[axis_at] // shards_of).reshape((-1,) + (1,) * (len(dims) - 1 - axis_at))
    return level


def split_up(amount, total, most, skew):
    loads = [(1 << 20) // math.isqrt(grade ** skew) + 1 for grade in range(2, amount + 1)]
    rest, given = total - most - (amount - 1), [1] * (amount - 1)
    while rest > 0:
        movable = [i for i in range(amount - 1) if given[i] < most]
        whole, left = sum([loads[i] for i in movable]), rest
        for i in movable:
            extra = min(most - given[i], max(1, left * loads[i] // whole), rest)
            given[i] = given[i] + extra
            rest = rest - extra
    return np.array([most] + given)


def ragged_sizes(own_key, number_of, total, most, lean):
    if number_of == 2:
        one = jax.random.randint(own_key, (), max(1, total - most), min(most, total - 1) + 1)
        return jnp.stack([one, total - one])
    lengths = jnp.asarray(split_up(number_of, total, most, lean), jnp.int32)
    couples = (number_of - 1) // 2
    donor, sink = lengths[1:1 + 2 * couples:2], lengths[2:2 + 2 * couples:2]
    room = jnp.minimum(donor - 1, most - sink)
    passed = jax.random.randint(jax.random.fold_in(own_key, 1), (couples,), 0, 1 << 20) % (room + 1)
    lengths = lengths.at[1:1 + 2 * couples:2].set(donor - passed).at[2:2 + 2 * couples:2].set(sink + passed)
    return lengths[jax.random.permutation(jax.random.fold_in(own_key, 2), number_of)]


def scatter_about(key, shape, width, bound, cuts=(), held_as=jnp.bfloat16):
    gain = level_of(key, shape, cuts, -0.22, 0.18) if cuts else 1.0
    result = jax.random.normal(key, shape, jnp.float32) * width * gain
    return jnp.minimum(jnp.maximum(result, -bound), bound).astype(held_as)


def setup_inputs(seed: int = 0) -> dict:
    splits = jax.random.split(jax.random.key(seed), 12)
    frame_cotangent = scatter_about(splits[0], (ROLLOUTS, SEQ, D), 0.35, 5.0, ((0, 8), (2, 4)))
    rollout_utterance = draw_rollout_utterance(jax.random.fold_in(splits[11], 71), 0)
    frame_offset = place_ends(jax.random.randint(splits[2], (ROLLOUTS,), 0, PROMPT + 1), jax.random.fold_in(splits[2], 1), 0, PROMPT).astype(jnp.int32)
    utterance_frames = ragged_sizes(splits[3], UTT, UTT * F * 3 // 4, F, 1).astype(jnp.int32)
    normed_input = scatter_about(splits[4], (UTT, F, C), 1.0, 6.0, ((0, 8), (2, 4)))
    expand_weight = scatter_about(splits[5], (C, 2, C), C ** -0.5, 0.1875, ((2, 4),))
    depth_kernel = scatter_about(splits[6], (K, C), K ** -0.5, 2.0, ((1, 4),))
    norm_scale = jnp.clip(1.0 + 0.18 * jax.random.normal(splits[7], (C,), jnp.float32), 0.1, 1.9)
    norm_shift = scatter_about(splits[8], (C,), 0.5, 3.0, ((0, 4),), jnp.float32)
    project_weight = scatter_about(splits[9], (C, C), C ** -0.5, 0.1875)
    adapter_weight = scatter_about(splits[10], (C, D), D ** -0.5, 0.0625, ((1, 4),))
    return {"frame_cotangent": frame_cotangent, "rollout_utterance": rollout_utterance, "frame_offset": frame_offset, "utterance_frames": utterance_frames, "normed_input": normed_input, "expand_weight": expand_weight, "depth_kernel": depth_kernel, "norm_scale": norm_scale, "norm_shift": norm_shift, "project_weight": project_weight, "adapter_weight": adapter_weight}


def reference(frame_cotangent, rollout_utterance, frame_offset, utterance_frames, normed_input, expand_weight, depth_kernel, norm_scale, norm_shift, project_weight, adapter_weight):
    grouped = frame_cotangent.reshape(N_DEC, R_DEV, SEQ, D)
    starts = frame_offset.astype(jnp.int32).reshape(N_DEC, R_DEV)
    owners = rollout_utterance.astype(jnp.int32).reshape(N_DEC, R_DEV)

    def per_device(total, item):
        rows, begin, utts = item
        slabs = jax.vmap(lambda window, first: lax.dynamic_slice_in_dim(window, first, F, 0))(rows, begin)
        part = jax.ops.segment_sum(slabs.astype(jnp.float32), utts, num_segments=UTT)
        rounded = lax.optimization_barrier(part.astype(jnp.bfloat16))
        return total + rounded.astype(jnp.float32), None

    total, _ = lax.scan(per_device, jnp.zeros((UTT, F, D), jnp.float32), (grouped, starts, owners))
    mask = (jnp.arange(F, dtype=jnp.int32)[None, :] < utterance_frames.astype(jnp.int32)[:, None]).astype(jnp.float32)
    frame_grad = (total * mask[:, :, None]).astype(jnp.bfloat16)
    grad_stream = jnp.dot(frame_grad.reshape(UTT * F, D), adapter_weight.T, preferred_element_type=jnp.float32).astype(jnp.bfloat16)

    expand_flat = expand_weight.reshape(C, 2 * C)
    expanded = jnp.dot(normed_input.reshape(UTT * F, C), expand_flat, preferred_element_type=jnp.float32)
    value = expanded[:, :C]
    gate = expanded[:, C:]
    sig_gate = jax.nn.sigmoid(gate)
    mask_rows = mask.reshape(UTT * F, 1)
    glu = (mask_rows * value * sig_gate).reshape(UTT, F, C)
    kernel = depth_kernel.astype(jnp.float32)
    half = (K - 1) // 2
    padded = jnp.pad(glu, ((0, 0), (half, half), (0, 0)))
    depth = jnp.zeros((UTT, F, C), jnp.float32)
    for k in range(K):
        depth = depth + kernel[k] * padded[:, k:k + F, :]
    shifted = depth * norm_scale + norm_shift
    grad_swish = jnp.dot(grad_stream, project_weight.T, preferred_element_type=jnp.float32).reshape(UTT, F, C)
    sig_shift = jax.nn.sigmoid(shifted)
    grad_depth = grad_swish * sig_shift * (1.0 + shifted * (1.0 - sig_shift)) * norm_scale
    padded_back = jnp.pad(grad_depth, ((0, 0), (half, half), (0, 0)))
    grad_glu = jnp.zeros((UTT, F, C), jnp.float32)
    for k in range(K):
        grad_glu = grad_glu + kernel[k] * padded_back[:, K - 1 - k:K - 1 - k + F, :]
    grad_glu = grad_glu.reshape(UTT * F, C) * mask_rows
    grad_value = grad_glu * sig_gate
    grad_gate = grad_glu * value * sig_gate * (1.0 - sig_gate)
    grad_expanded = jnp.concatenate([grad_value, grad_gate], axis=1).astype(jnp.bfloat16)
    grad_normed = jnp.dot(grad_expanded, expand_flat.T, preferred_element_type=jnp.float32).astype(jnp.bfloat16)
    return grad_stream.reshape(UTT, F, C), grad_normed.reshape(UTT, F, C)
```

```python
import functools

import jax
import jax.numpy as jnp
from jax import lax
from jax.experimental import pallas as pl
from jax.experimental.pallas import tpu as pltpu
from jax.sharding import PartitionSpec as P

F32 = jnp.float32
BF16 = jnp.bfloat16
NT = (((1,), (1,)), ((), ()))
NN = (((1,), (0,)), ((), ()))
ROW_TILE = 16
LANES = 128
COLS = 256
VMEM = pl.BlockSpec(memory_space=pltpu.VMEM)
SMEM = pl.BlockSpec(memory_space=pltpu.SMEM)


def dot(a, b, dims):
    return lax.dot_general(a, b, dims, preferred_element_type=F32)


def adapter_kernel(flip, frames, index, utts, offsets, windows, weight, out, slabs, product, sem):
    targets = out.shape[0]
    rolls, seq_len, _ = windows.shape
    span = slabs.shape[0] // targets
    dec = index[0]

    def pick(step):
        target = ((dec // 2) ^ step) * 2 + ((dec % 2) ^ flip)
        found, first = jnp.int32(-1), jnp.int32(0)
        for roll in range(rolls):
            hit = utts[roll] == target
            found = jnp.where(hit, roll, found)
            first = jnp.where(hit, offsets[roll], first)
        start = jnp.minimum(first // ROW_TILE * ROW_TILE, seq_len - span)
        return found, start, first - start

    picks = [pick(step) for step in range(targets)]

    def copy(step):
        found, start, _ = picks[step]
        return pltpu.make_async_copy(
            windows.at[jnp.maximum(found, 0), pl.ds(pl.multiple_of(start, ROW_TILE), span), :],
            slabs.at[pl.ds(step * span, span), :],
            sem.at[step],
        )

    @pl.when(pl.program_id(0) == 0)
    def _():
        for step in range(targets):
            copy(step).start()
        for step in range(targets):
            copy(step).wait()

    result = dot(slabs[...], weight[...], NT)
    for lane in range(COLS // LANES):
        product[lane, :, :] = result[:, lane * LANES : (lane + 1) * LANES]
    for step in range(targets):
        found, _, shift = picks[step]
        for lane in range(COLS // LANES):
            rows = product[lane, pl.ds(step * span + shift, frames), :]
            out[step, :, lane * LANES : (lane + 1) * LANES] = jnp.where(found >= 0, rows, 0.0).astype(BF16)


def adapter(flip, targets, frames, index, utts, offsets, windows, weight):
    rolls, seq_len, d_local = windows.shape
    width = weight.shape[0]
    span = frames + ROW_TILE
    return pl.pallas_call(
        functools.partial(adapter_kernel, flip, frames),
        grid=(width // COLS,),
        out_shape=jax.ShapeDtypeStruct((targets, frames, width), BF16),
        in_specs=[
            SMEM,
            SMEM,
            SMEM,
            pl.BlockSpec(memory_space=pl.ANY),
            pl.BlockSpec((COLS, d_local), lambda n: (n, 0)),
        ],
        out_specs=pl.BlockSpec((targets, frames, COLS), lambda n: (0, 0, n)),
        scratch_shapes=[
            pltpu.VMEM((targets * span, d_local), BF16),
            pltpu.VMEM((COLS // LANES, targets * span, LANES), F32),
            pltpu.SemaphoreType.DMA((targets,)),
        ],
        compiler_params=pltpu.CompilerParams(vmem_limit_bytes=24 << 20),
        cost_estimate=pl.CostEstimate(
            flops=2 * targets * span * d_local * width,
            bytes_accessed=2 * (targets * span * d_local + width * d_local + targets * frames * width),
            transcendentals=0,
        ),
        name="adapter_other" if flip else "adapter_own",
    )(index, utts, offsets, windows, weight)


def pair_sum_kernel(own, other, *outs):
    for step, out in enumerate(outs):
        out[...] = (own[step].astype(F32) + other[step].astype(F32)).astype(BF16)


def pair_sum(own, other):
    targets, frames, width = own.shape
    return pl.pallas_call(
        pair_sum_kernel,
        out_shape=[jax.ShapeDtypeStruct((frames, width), BF16)] * targets,
        in_specs=[VMEM] * 2,
        out_specs=[VMEM] * targets,
        compiler_params=pltpu.CompilerParams(vmem_limit_bytes=24 << 20),
        name="pair_sum",
    )(own, other)


def swish_kernel(parts, index, valid, project, *refs):
    blocks, outs, stream = refs[:parts], refs[parts:-1], refs[-1]
    frames, width = stream.shape
    c_local = outs[0].shape[1] // 2
    total = blocks[0][...].astype(F32)
    for block in blocks[1:]:
        total = total + block[...].astype(F32)
    rows = lax.broadcasted_iota(jnp.int32, (frames, width), 0)
    stream[...] = jnp.where(rows < valid[0], total, 0.0).astype(BF16)
    ch = index[1]
    for step, out in enumerate(outs):
        at = pl.ds(pl.multiple_of((ch ^ step) * c_local, c_local), c_local)
        out[:, :c_local] = stream[:, at].astype(out.dtype)
        out[:, c_local:] = dot(stream[...], project[at, :], NT).astype(out.dtype)


def swish(index, valid, project, blocks, groups):
    frames, width = blocks[0].shape
    c_local = width // groups
    return pl.pallas_call(
        functools.partial(swish_kernel, len(blocks)),
        out_shape=[jax.ShapeDtypeStruct((frames, 2 * c_local), F32 if step == 0 else BF16) for step in range(groups)],
        in_specs=[SMEM, SMEM, VMEM] + [VMEM] * len(blocks),
        out_specs=[VMEM] * groups,
        scratch_shapes=[pltpu.VMEM((frames, width), BF16)],
        compiler_params=pltpu.CompilerParams(vmem_limit_bytes=24 << 20),
        name="stream_and_swish",
    )(index, valid, project, *blocks)


def forward_kernel(parts, index, valid, expand, taps_ref, scale, shift, *refs):
    blocks, (value_out, gate_out, slope_out), padded = refs[:parts], refs[parts:-1], refs[-1]
    frames, c_local = value_out.shape
    taps = taps_ref.shape[0]
    half = (taps - 1) // 2
    ch = index[1]
    expanded = jnp.zeros((frames, 2 * c_local), F32)
    for step, block in enumerate(blocks):
        at = pl.ds(pl.multiple_of((ch ^ step) * c_local, c_local), c_local)
        expanded = expanded + dot(block[...], expand[at, :], NN)
    value = expanded[:, :c_local]
    gate = jax.nn.sigmoid(expanded[:, c_local:])
    rows = lax.broadcasted_iota(jnp.int32, (frames, c_local), 0)
    glu = jnp.where(rows < valid[0], value * gate, 0.0)
    edge = padded.shape[0] - frames
    padded[: edge // 2, :] = jnp.zeros((edge // 2, c_local), F32)
    padded[edge // 2 + frames :, :] = jnp.zeros((edge // 2, c_local), F32)
    padded[pl.ds(edge // 2, frames), :] = glu
    depth = jnp.zeros((frames, c_local), F32)
    for tap in range(taps):
        depth = depth + taps_ref[tap : tap + 1, :] * padded[pl.ds(edge // 2 - half + tap, frames), :]
    shifted = depth * scale[...] + shift[...]
    sig = jax.nn.sigmoid(shifted)
    value_out[...] = value
    gate_out[...] = gate
    slope_out[...] = sig * (1.0 + shifted * (1.0 - sig)) * scale[...]


def edge_of(taps):
    return 2 * (-(-((taps - 1) // 2) // 8) * 8)


def forward(index, valid, expand, taps, scale, shift, blocks):
    frames, c_local = blocks[0].shape
    return pl.pallas_call(
        functools.partial(forward_kernel, len(blocks)),
        out_shape=[jax.ShapeDtypeStruct((frames, c_local), F32)] * 3,
        in_specs=[SMEM, SMEM] + [VMEM] * (4 + len(blocks)),
        out_specs=[VMEM] * 3,
        scratch_shapes=[pltpu.VMEM((frames + edge_of(taps.shape[0]), c_local), F32)],
        compiler_params=pltpu.CompilerParams(vmem_limit_bytes=16 << 20),
        name="forward_gates",
    )(index, valid, expand, taps, scale, shift, *blocks)


def backward_kernel(parts, index, valid, expand, taps_ref, value_ref, gate_ref, slope, *refs):
    blocks, stream_out, outs, padded = refs[:parts], refs[parts], refs[parts + 1 : -1], refs[-1]
    frames, c_local = stream_out.shape
    taps = taps_ref.shape[0]
    half = (taps - 1) // 2
    ch = index[1]
    total = blocks[0][...].astype(F32)
    for block in blocks[1:]:
        total = total + block[...].astype(F32)
    stream_out[...] = total[:, :c_local].astype(BF16)
    edge = padded.shape[0] - frames
    padded[: edge // 2, :] = jnp.zeros((edge // 2, c_local), F32)
    padded[edge // 2 + frames :, :] = jnp.zeros((edge // 2, c_local), F32)
    padded[pl.ds(edge // 2, frames), :] = total[:, c_local:] * slope[...]
    grad = jnp.zeros((frames, c_local), F32)
    for tap in range(taps):
        grad = grad + taps_ref[tap : tap + 1, :] * padded[pl.ds(edge // 2 + half - tap, frames), :]
    rows = lax.broadcasted_iota(jnp.int32, (frames, c_local), 0)
    grad = jnp.where(rows < valid[0], grad, 0.0)
    gate = gate_ref[...]
    grad_value = grad * gate
    grad_gate = grad_value * value_ref[...] * (1.0 - gate)
    grad_expanded = jnp.concatenate([grad_value.astype(BF16), grad_gate.astype(BF16)], axis=1)
    for step, out in enumerate(outs):
        at = pl.ds(pl.multiple_of((ch ^ step) * c_local, c_local), c_local)
        out[...] = dot(grad_expanded, expand[at, :], NT).astype(out.dtype)


def backward(index, valid, expand, taps, value, gate, slope, blocks, groups):
    frames, c_local = value.shape
    return pl.pallas_call(
        functools.partial(backward_kernel, len(blocks)),
        out_shape=[jax.ShapeDtypeStruct((frames, c_local), BF16)]
        + [jax.ShapeDtypeStruct((frames, c_local), F32 if step == 0 else BF16) for step in range(groups)],
        in_specs=[SMEM, SMEM] + [VMEM] * (5 + len(blocks)),
        out_specs=[VMEM] * (1 + groups),
        scratch_shapes=[pltpu.VMEM((frames + edge_of(taps.shape[0]), c_local), F32)],
        compiler_params=pltpu.CompilerParams(vmem_limit_bytes=16 << 20),
        name="backward_module",
    )(index, valid, expand, taps, value, gate, slope, *blocks)


def swap(block, axis, count, mask):
    return lax.ppermute(block, axis, [(i, i ^ mask) for i in range(count)])


def body(
    n_dec,
    n_ch,
    frame_cotangent,
    rollout_utterance,
    frame_offset,
    utterance_frames,
    normed_input,
    expand_weight,
    depth_kernel,
    norm_scale,
    norm_shift,
    project_weight,
    adapter_weight,
):
    u_local, frames, c_local = normed_input.shape
    width = expand_weight.shape[0]
    chips = n_dec // 2
    index = jnp.stack([lax.axis_index("dec"), lax.axis_index("ch")]).astype(jnp.int32)
    own_input = normed_input.reshape(frames, c_local)
    inputs = [own_input] + [swap(own_input, "ch", n_ch, step) for step in range(1, n_ch)]
    expand = expand_weight.reshape(width, 2 * c_local)
    taps = depth_kernel.astype(F32)
    scale, shift = norm_scale.reshape(1, c_local), norm_shift.reshape(1, c_local)

    route = (index, rollout_utterance, frame_offset, frame_cotangent, adapter_weight)
    for_other = adapter(1, chips, frames, *route)
    from_other = swap(for_other, "dec", n_dec, 1)
    own = adapter(0, chips, frames, *route)
    sums = pair_sum(own, from_other)
    arrived = [sums[0]] + [swap(sums[step], "dec", n_dec, 2 * step) for step in reversed(range(1, chips))]
    value, gate, slope = forward(index, utterance_frames, expand, taps, scale, shift, inputs)
    halves = swish(index, utterance_frames, project_weight, arrived, n_ch)
    halves = [halves[0]] + [swap(halves[step], "ch", n_ch, step) for step in range(1, n_ch)]
    stream, *parts = backward(index, utterance_frames, expand, taps, value, gate, slope, halves, n_ch)
    total = parts[0]
    for step in range(1, n_ch):
        total = total + swap(parts[step], "ch", n_ch, step).astype(F32)
    return stream[None], total.astype(BF16)[None]


def solution(mesh):
    return jax.shard_map(
        functools.partial(body, mesh.shape["dec"], mesh.shape["ch"]),
        mesh=mesh,
        in_specs=(
            P("dec", None, "ch"),
            P("dec"),
            P("dec"),
            P("dec"),
            P("dec", None, "ch"),
            P(None, None, "ch"),
            P(None, "ch"),
            P("ch"),
            P("ch"),
            P(),
            P(None, "ch"),
        ),
        out_specs=(P("dec", None, "ch"), P("dec", None, "ch")),
        check_vma=False,
    )
```

```python
import functools

import jax
import jax.numpy as jnp
from jax import lax
from jax.experimental import pallas as pl
from jax.experimental.pallas import tpu as pltpu
from jax.sharding import PartitionSpec as P

F32 = jnp.float32
BF16 = jnp.bfloat16
NT = (((1,), (1,)), ((), ()))
NN = (((1,), (0,)), ((), ()))
ROW_TILE = 16
LANES = 128
COLS = 256
VMEM = pl.BlockSpec(memory_space=pltpu.VMEM)
SMEM = pl.BlockSpec(memory_space=pltpu.SMEM)
HBM = pl.BlockSpec(memory_space=pltpu.HBM)
HALVES = 2
OTHER_VMEM = 48
OWN_VMEM = 48


def dot(a, b, dims):
    return lax.dot_general(a, b, dims, preferred_element_type=F32)


def matmul_cost(rows, depth, columns):
    return pl.CostEstimate(
        flops=2 * rows * depth * columns,
        bytes_accessed=2 * (rows * depth + depth * columns + rows * columns),
        transcendentals=0,
    )


def picks_of(meta, flip, targets, last_start):
    dec = lax.axis_index("dec")
    picks = []
    for step in range(targets):
        target = ((dec // 2) ^ step) * 2 + ((dec % 2) ^ flip)
        found, first = jnp.int32(-1), jnp.int32(0)
        for roll in range(meta.shape[1]):
            hit = meta[0, roll] == target
            found = jnp.where(hit, roll, found)
            first = jnp.where(hit, meta[1, roll], first)
        start = jnp.minimum(first // ROW_TILE * ROW_TILE, last_start)
        picks.append((found, start, first - start))
    return picks


def multiply(slabs, rows, product):
    result = dot(slabs[...], rows[...], NT)
    for lane in range(COLS // LANES):
        product[lane, :, :] = result[:, lane * LANES : (lane + 1) * LANES]


def cut_rows(product, out, picks, chunk):
    targets, frames, _ = out.shape
    span = product.shape[1] // targets
    for step in range(targets):
        found, _, shift = picks[step]
        for lane in range(COLS // LANES):
            rows = product[lane, pl.ds(step * span + shift, frames), :]
            at = chunk * COLS + lane * LANES
            out[step, :, at : at + LANES] = jnp.where(found >= 0, rows, 0.0).astype(BF16)


def weight_copies(weight_hbm, head, tail, sem):
    return [
        pltpu.make_async_copy(
            weight_hbm.at[pl.ds(chunk * COLS, COLS), :],
            tail.at[pl.ds((chunk - 1) * COLS, COLS), :] if chunk else head,
            sem.at[chunk],
        )
        for chunk in range(weight_hbm.shape[0] // COLS)
    ]


def other_kernel(routes, windows, weight, out, own, head, meta, slabs, tail, *refs):
    products, (meta_sem, sem, weight_sem) = refs[:2], refs[2:]
    targets = out.shape[0]
    span = slabs.shape[0] // targets
    last_start = windows.shape[1] - span

    def slab_copies(flip, picks, held):
        return [
            pltpu.make_async_copy(
                windows.at[jnp.maximum(found, 0), pl.ds(pl.multiple_of(start, ROW_TILE), span), :],
                held.at[pl.ds(step * span, span), :],
                sem.at[flip, step],
            )
            for step, (found, start, _) in enumerate(picks)
        ]

    route_copy = pltpu.make_async_copy(routes, meta, meta_sem)
    weights = weight_copies(weight, head, tail, weight_sem)
    route_copy.start()
    weights[0].start()
    route_copy.wait()
    picks = picks_of(meta, 1, targets, last_start)
    copies = slab_copies(1, picks, slabs)
    own_copies = slab_copies(0, picks_of(meta, 0, targets, last_start), own)
    for copy in copies + weights[1:] + own_copies:
        copy.start()
    for copy in copies:
        copy.wait()
    for chunk, copy in enumerate(weights):
        copy.wait()
        multiply(slabs, tail.at[pl.ds((chunk - 1) * COLS, COLS), :] if chunk else head, products[chunk % 2])
        cut_rows(products[chunk % 2], out, picks, chunk)
    for copy in own_copies:
        copy.wait()


def adapter_other(frames, routes, windows, weight):
    _, _, d_local = windows.shape
    width = weight.shape[0]
    targets = lax.axis_size("dec") // 2
    span = frames + ROW_TILE
    return pl.pallas_call(
        other_kernel,
        out_shape=[
            jax.ShapeDtypeStruct((targets, frames, width), BF16),
            jax.ShapeDtypeStruct((targets * span, d_local), BF16),
            jax.ShapeDtypeStruct((COLS, d_local), BF16),
        ],
        in_specs=[HBM] * 3,
        out_specs=[VMEM] * 3,
        scratch_shapes=[
            pltpu.SMEM(routes.shape, jnp.int32),
            pltpu.VMEM((targets * span, d_local), BF16),
            pltpu.VMEM((width - COLS, d_local), BF16),
            pltpu.VMEM((COLS // LANES, targets * span, LANES), F32),
            pltpu.VMEM((COLS // LANES, targets * span, LANES), F32),
            pltpu.SemaphoreType.DMA,
            pltpu.SemaphoreType.DMA((2, targets)),
            pltpu.SemaphoreType.DMA((width // COLS,)),
        ],
        compiler_params=pltpu.CompilerParams(vmem_limit_bytes=OTHER_VMEM << 20),
        cost_estimate=matmul_cost(targets * span, d_local, width),
        name="adapter_other",
    )(routes, windows, weight)


def own_kernel(last_start, routes, slabs, head, weight, out, meta, tail, *refs):
    products, (meta_sem, weight_sem) = refs[:2], refs[2:]
    route_copy = pltpu.make_async_copy(routes, meta, meta_sem)
    weights = weight_copies(weight, head, tail, weight_sem)[1:]
    route_copy.start()
    for copy in weights:
        copy.start()
    multiply(slabs, head, products[0])
    route_copy.wait()
    picks = picks_of(meta, 0, out.shape[0], last_start)
    for chunk, copy in enumerate(weights):
        copy.wait()
        multiply(slabs, tail.at[pl.ds(chunk * COLS, COLS), :], products[(chunk + 1) % 2])
        cut_rows(products[chunk % 2], out, picks, chunk)
    cut_rows(products[len(weights) % 2], out, picks, len(weights))


def adapter_own(frames, seq_len, routes, slabs, head, weight):
    width, d_local = weight.shape
    targets = lax.axis_size("dec") // 2
    span = frames + ROW_TILE
    return pl.pallas_call(
        functools.partial(own_kernel, seq_len - span),
        out_shape=jax.ShapeDtypeStruct((targets, frames, width), BF16),
        in_specs=[HBM] + [VMEM] * 2 + [HBM],
        out_specs=VMEM,
        scratch_shapes=[
            pltpu.SMEM(routes.shape, jnp.int32),
            pltpu.VMEM((width - COLS, d_local), BF16),
            pltpu.VMEM((COLS // LANES, targets * span, LANES), F32),
            pltpu.VMEM((COLS // LANES, targets * span, LANES), F32),
            pltpu.SemaphoreType.DMA,
            pltpu.SemaphoreType.DMA((width // COLS,)),
        ],
        compiler_params=pltpu.CompilerParams(vmem_limit_bytes=OWN_VMEM << 20),
        cost_estimate=matmul_cost(targets * span, d_local, width),
        name="adapter_own",
    )(routes, slabs, head, weight)


def pair_sum_kernel(own, other, *outs):
    targets, frames, _ = own.shape
    size = frames // HALVES
    for at, out in enumerate(outs):
        half, step = divmod(at, targets)
        rows = pl.ds(half * size, size)
        out[...] = (own[step, rows, :].astype(F32) + other[step, rows, :].astype(F32)).astype(BF16)


def pair_sum(own, other):
    targets, frames, width = own.shape
    outs = pl.pallas_call(
        pair_sum_kernel,
        out_shape=[jax.ShapeDtypeStruct((frames // HALVES, width), BF16)] * (targets * HALVES),
        in_specs=[VMEM] * 2,
        out_specs=[VMEM] * (targets * HALVES),
        compiler_params=pltpu.CompilerParams(vmem_limit_bytes=24 << 20),
        name="pair_sum",
    )(own, other)
    return [outs[half * targets : (half + 1) * targets] for half in range(HALVES)]


def swish_kernel(parts, first, valid, project, *refs):
    blocks, outs, stream = refs[:parts], refs[parts:-1], refs[-1]
    frames, width = stream.shape
    c_local = outs[0].shape[1] // 2
    total = blocks[0][...].astype(F32)
    for block in blocks[1:]:
        total = total + block[...].astype(F32)
    rows = first + lax.broadcasted_iota(jnp.int32, (frames, width), 0)
    stream[...] = jnp.where(rows < valid[0], total, 0.0).astype(BF16)
    ch = lax.axis_index("ch")
    for step, out in enumerate(outs):
        at = pl.ds(pl.multiple_of((ch ^ step) * c_local, c_local), c_local)
        out[:, :c_local] = stream[:, at].astype(out.dtype)
        out[:, c_local:] = dot(stream[...], project[step], NN).astype(out.dtype)


def swish(first, valid, project, blocks):
    frames, width = blocks[0].shape
    groups, _, c_local = project.shape
    return pl.pallas_call(
        functools.partial(swish_kernel, len(blocks), first),
        out_shape=[jax.ShapeDtypeStruct((frames, 2 * c_local), F32 if step == 0 else BF16) for step in range(groups)],
        in_specs=[SMEM, VMEM] + [VMEM] * len(blocks),
        out_specs=[VMEM] * groups,
        scratch_shapes=[pltpu.VMEM((frames, width), BF16)],
        compiler_params=pltpu.CompilerParams(vmem_limit_bytes=24 << 20),
        cost_estimate=matmul_cost(frames, width, width),
        name="stream_and_swish",
    )(valid, project, *blocks)


def spread_rows(padded, rows):
    frames, c_local = rows.shape
    edge = (padded.shape[0] - frames) // 2
    padded[:edge, :] = jnp.zeros((edge, c_local), F32)
    padded[edge + frames :, :] = jnp.zeros((edge, c_local), F32)
    padded[pl.ds(edge, frames), :] = rows


def edge_of(taps):
    return -(-((taps - 1) // 2) // 8) * 8


def forward_kernel(parts, valid, expand, project, taps_ref, scale, shift, *refs):
    blocks, (value_out, gate_out, slope_out, project_t, expand_t, padded) = refs[:parts], refs[parts:]
    frames, c_local = value_out.shape
    taps = taps_ref.shape[0]
    half = (taps - 1) // 2
    edge = (padded.shape[0] - frames) // 2
    ch = lax.axis_index("ch")
    expanded = jnp.zeros((frames, 2 * c_local), F32)
    for step, block in enumerate(blocks):
        at = pl.ds(pl.multiple_of((ch ^ step) * c_local, c_local), c_local)
        expanded = expanded + dot(block[...], expand[at, :], NN)
        project_t[step, :, :] = project[at, :].T
        expand_t[step, :, :] = expand[at, :].T
    value = expanded[:, :c_local]
    gate = jax.nn.sigmoid(expanded[:, c_local:])
    rows = lax.broadcasted_iota(jnp.int32, (frames, c_local), 0)
    spread_rows(padded, jnp.where(rows < valid[0], value * gate, 0.0))
    depth = jnp.zeros((frames, c_local), F32)
    for tap in range(taps):
        depth = depth + taps_ref[tap : tap + 1, :] * padded[pl.ds(edge - half + tap, frames), :]
    shifted = depth * scale[...] + shift[...]
    sig = jax.nn.sigmoid(shifted)
    value_out[...] = value
    gate_out[...] = gate
    slope_out[...] = sig * (1.0 + shifted * (1.0 - sig)) * scale[...]


def forward(valid, expand, project, taps, scale, shift, blocks):
    frames, c_local = blocks[0].shape
    groups, width = len(blocks), project.shape[1]
    return pl.pallas_call(
        functools.partial(forward_kernel, groups),
        out_shape=[jax.ShapeDtypeStruct((frames, c_local), F32)] * 3
        + [jax.ShapeDtypeStruct((groups, width, c_local), BF16), jax.ShapeDtypeStruct((groups, 2 * c_local, c_local), BF16)],
        in_specs=[SMEM] + [VMEM] * (5 + groups),
        out_specs=[VMEM] * 5,
        scratch_shapes=[pltpu.VMEM((frames + 2 * edge_of(taps.shape[0]), c_local), F32)],
        compiler_params=pltpu.CompilerParams(vmem_limit_bytes=24 << 20),
        cost_estimate=matmul_cost(frames, 4 * width, 2 * c_local),
        name="forward_gates",
    )(valid, expand, project, taps, scale, shift, *blocks)


def backward_kernel(parts, valid, expand_t, taps_ref, value_ref, gate_ref, slope, *refs):
    blocks, stream_out, outs, padded = refs[: parts * HALVES], refs[parts * HALVES], refs[parts * HALVES + 1 : -1], refs[-1]
    frames, c_local = stream_out.shape
    size = frames // HALVES
    taps = taps_ref.shape[0]
    half = (taps - 1) // 2
    edge = (padded.shape[0] - frames) // 2
    spread_rows(padded, jnp.zeros((frames, c_local), F32))
    for at in range(HALVES):
        total = blocks[at * parts][...].astype(F32)
        for block in blocks[at * parts + 1 : (at + 1) * parts]:
            total = total + block[...].astype(F32)
        rows = pl.ds(at * size, size)
        stream_out[rows, :] = total[:, :c_local].astype(BF16)
        padded[pl.ds(edge + at * size, size), :] = total[:, c_local:] * slope[rows, :]
    grad = jnp.zeros((frames, c_local), F32)
    for tap in range(taps):
        grad = grad + taps_ref[tap : tap + 1, :] * padded[pl.ds(edge + half - tap, frames), :]
    rows = lax.broadcasted_iota(jnp.int32, (frames, c_local), 0)
    grad = jnp.where(rows < valid[0], grad, 0.0)
    gate = gate_ref[...]
    grad_value = grad * gate
    grad_gate = grad_value * value_ref[...] * (1.0 - gate)
    grad_expanded = jnp.concatenate([grad_value.astype(BF16), grad_gate.astype(BF16)], axis=1)
    for step, out in enumerate(outs):
        out[...] = dot(grad_expanded, expand_t[step], NN).astype(out.dtype)


def backward(valid, expand_t, taps, value, gate, slope, halves):
    frames, c_local = value.shape
    groups = expand_t.shape[0]
    return pl.pallas_call(
        functools.partial(backward_kernel, groups),
        out_shape=[jax.ShapeDtypeStruct((frames, c_local), BF16)]
        + [jax.ShapeDtypeStruct((frames, c_local), F32 if step == 0 else BF16) for step in range(groups)],
        in_specs=[SMEM] + [VMEM] * (5 + groups * HALVES),
        out_specs=[VMEM] * (1 + groups),
        scratch_shapes=[pltpu.VMEM((frames + 2 * edge_of(taps.shape[0]), c_local), F32)],
        compiler_params=pltpu.CompilerParams(vmem_limit_bytes=16 << 20),
        cost_estimate=matmul_cost(frames, 2 * c_local, c_local * groups),
        name="backward_module",
    )(valid, expand_t, taps, value, gate, slope, *[block for half in halves for block in half])


def swap(block, axis, count, mask):
    return lax.ppermute(block, axis, [(i, i ^ mask) for i in range(count)])


def body(
    n_dec,
    n_ch,
    frame_cotangent,
    rollout_utterance,
    frame_offset,
    utterance_frames,
    normed_input,
    expand_weight,
    depth_kernel,
    norm_scale,
    norm_shift,
    project_weight,
    adapter_weight,
):
    u_local, frames, c_local = normed_input.shape
    width = expand_weight.shape[0]
    chips = n_dec // 2
    own_input = normed_input.reshape(frames, c_local)
    inputs = [own_input] + [swap(own_input, "ch", n_ch, step) for step in range(1, n_ch)]
    expand = expand_weight.reshape(width, 2 * c_local)
    taps = depth_kernel.astype(F32)
    scale, shift = norm_scale.reshape(1, c_local), norm_shift.reshape(1, c_local)

    seq_len = frame_cotangent.shape[1]
    routes = jnp.stack([rollout_utterance, frame_offset])
    for_other, own_slabs, head = adapter_other(frames, routes, frame_cotangent, adapter_weight)
    from_other = swap(for_other, "dec", n_dec, 1)
    own = adapter_own(frames, seq_len, routes, own_slabs, head, adapter_weight)
    own, inputs = lax.optimization_barrier((own, inputs))
    sums = pair_sum(own, from_other)
    arrived = [
        [half[0]] + [swap(half[step], "dec", n_dec, 2 * step) for step in reversed(range(1, chips))] for half in sums
    ]
    value, gate, slope, project_t, expand_t = forward(
        utterance_frames, expand, project_weight, taps, scale, shift, inputs
    )
    halves = []
    for at, half in enumerate(arrived):
        sent = swish(at * frames // HALVES, utterance_frames, project_t, half)
        halves.append([sent[0]] + [swap(sent[step], "ch", n_ch, step) for step in range(1, n_ch)])
    stream, *parts = backward(utterance_frames, expand_t, taps, value, gate, slope, halves)
    total = parts[0]
    for step in range(1, n_ch):
        total = total + swap(parts[step], "ch", n_ch, step).astype(F32)
    return stream[None], total.astype(BF16)[None]


def solution(mesh):
    return jax.shard_map(
        functools.partial(body, mesh.shape["dec"], mesh.shape["ch"]),
        mesh=mesh,
        in_specs=(
            P("dec", None, "ch"),
            P("dec"),
            P("dec"),
            P("dec"),
            P("dec", None, "ch"),
            P(None, None, "ch"),
            P(None, "ch"),
            P("ch"),
            P("ch"),
            P(),
            P(None, "ch"),
        ),
        out_specs=(P("dec", None, "ch"), P("dec", None, "ch")),
        check_vma=False,
    )
```

```python
import functools

import jax
import jax.numpy as jnp
from jax import lax
from jax.experimental import pallas as pl
from jax.experimental.pallas import tpu as pltpu
from jax.sharding import PartitionSpec as P

F32 = jnp.float32
BF16 = jnp.bfloat16
NT = (((1,), (1,)), ((), ()))
NN = (((1,), (0,)), ((), ()))
ROW_TILE = 16
LANES = 128
PIECES = 2
VMEM = pl.BlockSpec(memory_space=pltpu.VMEM)
SMEM = pl.BlockSpec(memory_space=pltpu.SMEM)
HBM = pl.BlockSpec(memory_space=pltpu.HBM)
HALVES = 2
OTHER_VMEM = 45
OWN_VMEM = 24


def dot(a, b, dims):
    return lax.dot_general(a, b, dims, preferred_element_type=F32)


def matmul_cost(rows, depth, columns):
    return pl.CostEstimate(
        flops=2 * rows * depth * columns,
        bytes_accessed=2 * (rows * depth + depth * columns + rows * columns),
        transcendentals=0,
    )


def picks_of(meta, flip, targets, last_start):
    dec = lax.axis_index("dec")
    picks = []
    for step in range(targets):
        target = ((dec // 2) ^ step) * 2 + ((dec % 2) ^ flip)
        found, first = jnp.int32(-1), jnp.int32(0)
        for roll in range(meta.shape[1]):
            hit = meta[0, roll] == target
            found = jnp.where(hit, roll, found)
            first = jnp.where(hit, meta[1, roll], first)
        start = jnp.minimum(first // ROW_TILE * ROW_TILE, last_start)
        picks.append((found, start, first - start))
    return picks


def multiply(slabs, rows, product):
    for lane in range(0, product.shape[0], 2):
        result = dot(slabs[...], rows[lane * LANES : (lane + 2) * LANES, :], NT)
        product[lane, :, :] = result[:, :LANES]
        product[lane + 1, :, :] = result[:, LANES:]


def cut_rows(product, out, picks, first):
    targets, frames, _ = out.shape
    span = product.shape[1] // targets
    for lane in range(product.shape[0]):
        for step in range(targets):
            found, _, shift = picks[step]
            rows = product[lane, pl.ds(step * span + shift, frames), :]
            at = first + lane * LANES
            out[step, :, at : at + LANES] = jnp.where(found >= 0, rows, 0.0).astype(BF16)


def other_kernel(routes, windows, weight_hbm, out, own, weight, meta, slabs, *refs):
    products, (meta_sem, sem, weight_sem) = refs[:PIECES], refs[PIECES:]
    targets = out.shape[0]
    span = slabs.shape[0] // targets
    last_start = windows.shape[1] - span
    columns = weight.shape[0] // PIECES

    def slab_copies(flip, picks, held):
        return [
            pltpu.make_async_copy(
                windows.at[jnp.maximum(found, 0), pl.ds(pl.multiple_of(start, ROW_TILE), span), :],
                held.at[pl.ds(step * span, span), :],
                sem.at[flip, step],
            )
            for step, (found, start, _) in enumerate(picks)
        ]

    route_copy = pltpu.make_async_copy(routes, meta, meta_sem)
    route_copy.start()
    weights = []
    for piece in range(PIECES):
        at = pl.ds(piece * columns, columns)
        weights.append(pltpu.make_async_copy(weight_hbm.at[at, :], weight.at[at, :], weight_sem.at[piece]))
    weights[0].start()
    route_copy.wait()
    picks = picks_of(meta, 1, targets, last_start)
    copies = slab_copies(1, picks, slabs)
    own_copies = slab_copies(0, picks_of(meta, 0, targets, last_start), own)
    for copy in copies + weights[1:] + own_copies:
        copy.start()
    for copy in copies:
        copy.wait()
    for piece, copy in enumerate(weights):
        copy.wait()
        multiply(slabs, weight.at[pl.ds(piece * columns, columns), :], products[piece])
        cut_rows(products[piece], out, picks, piece * columns)
    for copy in own_copies:
        copy.wait()


def adapter_other(frames, routes, windows, weight):
    _, _, d_local = windows.shape
    width = weight.shape[0]
    targets = lax.axis_size("dec") // 2
    span = frames + ROW_TILE
    return pl.pallas_call(
        other_kernel,
        out_shape=[
            jax.ShapeDtypeStruct((targets, frames, width), BF16),
            jax.ShapeDtypeStruct((targets * span, d_local), BF16),
            jax.ShapeDtypeStruct((width, d_local), BF16),
        ],
        in_specs=[HBM] * 3,
        out_specs=[VMEM] * 3,
        scratch_shapes=[
            pltpu.SMEM(routes.shape, jnp.int32),
            pltpu.VMEM((targets * span, d_local), BF16),
        ]
        + [pltpu.VMEM((width // PIECES // LANES, targets * span, LANES), F32)] * PIECES
        + [
            pltpu.SemaphoreType.DMA,
            pltpu.SemaphoreType.DMA((2, targets)),
            pltpu.SemaphoreType.DMA((PIECES,)),
        ],
        compiler_params=pltpu.CompilerParams(vmem_limit_bytes=OTHER_VMEM << 20),
        cost_estimate=matmul_cost(targets * span, d_local, width),
        name="adapter_other",
    )(routes, windows, weight)


def own_kernel(last_start, routes, slabs, weight, out, meta, *refs):
    products, meta_sem = refs[:-1], refs[-1]
    columns = weight.shape[0] // len(products)
    route_copy = pltpu.make_async_copy(routes, meta, meta_sem)
    route_copy.start()
    multiply(slabs, weight.at[pl.ds(0, columns), :], products[0])
    route_copy.wait()
    picks = picks_of(meta, 0, out.shape[0], last_start)
    for piece, product in enumerate(products):
        if piece:
            multiply(slabs, weight.at[pl.ds(piece * columns, columns), :], product)
        cut_rows(product, out, picks, piece * columns)


def adapter_own(frames, seq_len, routes, slabs, weight):
    width, d_local = weight.shape
    targets = lax.axis_size("dec") // 2
    span = frames + ROW_TILE
    return pl.pallas_call(
        functools.partial(own_kernel, seq_len - span),
        out_shape=jax.ShapeDtypeStruct((targets, frames, width), BF16),
        in_specs=[HBM] + [VMEM] * 2,
        out_specs=VMEM,
        scratch_shapes=[pltpu.SMEM(routes.shape, jnp.int32)]
        + [pltpu.VMEM((width // PIECES // LANES, targets * span, LANES), F32)] * PIECES
        + [pltpu.SemaphoreType.DMA],
        compiler_params=pltpu.CompilerParams(vmem_limit_bytes=OWN_VMEM << 20),
        cost_estimate=matmul_cost(1, 1, 1),
        name="adapter_own",
    )(routes, slabs, weight)


def pair_sum_kernel(own, other, *outs):
    targets, frames, _ = own.shape
    size = frames // HALVES
    for at, out in enumerate(outs):
        half, step = divmod(at, targets)
        rows = pl.ds(half * size, size)
        out[...] = (own[step, rows, :].astype(F32) + other[step, rows, :].astype(F32)).astype(BF16)


def pair_sum(own, other):
    targets, frames, width = own.shape
    outs = pl.pallas_call(
        pair_sum_kernel,
        out_shape=[jax.ShapeDtypeStruct((frames // HALVES, width), BF16)] * (targets * HALVES),
        in_specs=[VMEM] * 2,
        out_specs=[VMEM] * (targets * HALVES),
        compiler_params=pltpu.CompilerParams(vmem_limit_bytes=24 << 20),
        name="pair_sum",
    )(own, other)
    return [outs[half * targets : (half + 1) * targets] for half in range(HALVES)]


def swish_kernel(parts, first, valid, project, *refs):
    blocks, outs, stream = refs[:parts], refs[parts:-1], refs[-1]
    frames, width = stream.shape
    c_local = outs[0].shape[1] // 2
    total = blocks[0][...].astype(F32)
    for block in blocks[1:]:
        total = total + block[...].astype(F32)
    rows = first + lax.broadcasted_iota(jnp.int32, (frames, width), 0)
    stream[...] = jnp.where(rows < valid[0], total, 0.0).astype(BF16)
    for step, out in enumerate(outs):
        at = pl.ds(pl.multiple_of(partner(step, len(outs)) * c_local, c_local), c_local)
        out[:, :c_local] = stream[:, at].astype(out.dtype)
        out[:, c_local:] = dot(stream[...], project[step], NN).astype(out.dtype)


def swish(first, valid, project, blocks):
    frames, width = blocks[0].shape
    groups, _, c_local = project.shape
    return pl.pallas_call(
        functools.partial(swish_kernel, len(blocks), first),
        out_shape=[jax.ShapeDtypeStruct((frames, 2 * c_local), F32 if step == 0 else BF16) for step in range(groups)],
        in_specs=[SMEM, VMEM] + [VMEM] * len(blocks),
        out_specs=[VMEM] * groups,
        scratch_shapes=[pltpu.VMEM((frames, width), BF16)],
        compiler_params=pltpu.CompilerParams(vmem_limit_bytes=24 << 20),
        cost_estimate=matmul_cost(frames, width, width),
        name="stream_and_swish",
    )(valid, project, *blocks)


def spread_rows(padded, rows):
    frames, c_local = rows.shape
    edge = (padded.shape[0] - frames) // 2
    padded[:edge, :] = jnp.zeros((edge, c_local), F32)
    padded[edge + frames :, :] = jnp.zeros((edge, c_local), F32)
    padded[pl.ds(edge, frames), :] = rows


def edge_of(taps):
    return -(-((taps - 1) // 2) // 8) * 8


def transpose_kernel(expand, project, expand_t, project_t):
    groups, _, c_local = project_t.shape
    for step in range(groups):
        at = pl.ds(pl.multiple_of(partner(step, groups) * c_local, c_local), c_local)
        project_t[step, :, :] = project[at, :].T
        expand_t[step, :, :] = expand[at, :].T


def transposed(groups, expand, project):
    width, span = expand.shape
    c_local = width // groups
    return pl.pallas_call(
        transpose_kernel,
        out_shape=[
            jax.ShapeDtypeStruct((groups, span, c_local), BF16),
            jax.ShapeDtypeStruct((groups, width, c_local), BF16),
        ],
        in_specs=[VMEM] * 2,
        out_specs=[VMEM] * 2,
        compiler_params=pltpu.CompilerParams(vmem_limit_bytes=24 << 20),
        cost_estimate=matmul_cost(128, width, 3 * c_local),
        name="transposed_weights",
    )(expand, project)


def forward_kernel(valid, expand, taps_ref, scale, shift, inputs, value_out, gate_out, slope_out, padded):
    frames, c_local = value_out.shape
    taps = taps_ref.shape[0]
    half = (taps - 1) // 2
    edge = (padded.shape[0] - frames) // 2
    expanded = jnp.zeros((frames, 2 * c_local), F32)
    masks = [0]
    while len(masks) * frames < inputs.shape[0]:
        far = inputs.shape[0] // frames // 2 // len(masks)
        masks += [mask ^ far for mask in masks]
    for place, mask in enumerate(masks):
        at = pl.ds(pl.multiple_of((lax.axis_index("ch") ^ mask) * c_local, c_local), c_local)
        expanded = expanded + dot(inputs[place * frames : (place + 1) * frames, :], expand[at, :], NN)
    value = expanded[:, :c_local]
    gate = jax.nn.sigmoid(expanded[:, c_local:])
    rows = lax.broadcasted_iota(jnp.int32, (frames, c_local), 0)
    spread_rows(padded, jnp.where(rows < valid[0], value * gate, 0.0))
    depth = jnp.zeros((frames, c_local), F32)
    for tap in range(taps):
        depth = depth + taps_ref[tap : tap + 1, :] * padded[pl.ds(edge - half + tap, frames), :]
    shifted = depth * scale[...] + shift[...]
    sig = jax.nn.sigmoid(shifted)
    value_out[...] = value
    gate_out[...] = gate
    slope_out[...] = sig * (1.0 + shifted * (1.0 - sig)) * scale[...]


def forward(frames, valid, expand, taps, scale, shift, inputs):
    width, c_local = expand.shape[0], inputs.shape[1]
    return pl.pallas_call(
        forward_kernel,
        out_shape=[jax.ShapeDtypeStruct((frames, c_local), F32)] * 3,
        in_specs=[SMEM] + [VMEM] * 5,
        out_specs=[VMEM] * 3,
        scratch_shapes=[pltpu.VMEM((frames + 2 * edge_of(taps.shape[0]), c_local), F32)],
        compiler_params=pltpu.CompilerParams(vmem_limit_bytes=24 << 20),
        cost_estimate=matmul_cost(frames, width, 2 * c_local),
        name="forward_gates",
    )(valid, expand, taps, scale, shift, inputs)


def backward_kernel(parts, valid, expand_t, taps_ref, value_ref, gate_ref, slope, *refs):
    blocks, stream_out, outs, padded = refs[: parts * HALVES], refs[parts * HALVES], refs[parts * HALVES + 1 : -1], refs[-1]
    frames, c_local = stream_out.shape
    size = frames // HALVES
    taps = taps_ref.shape[0]
    half = (taps - 1) // 2
    edge = (padded.shape[0] - frames) // 2
    spread_rows(padded, jnp.zeros((frames, c_local), F32))
    for at in range(HALVES):
        total = blocks[at * parts][...].astype(F32)
        for block in blocks[at * parts + 1 : (at + 1) * parts]:
            total = total + block[...].astype(F32)
        rows = pl.ds(at * size, size)
        stream_out[rows, :] = total[:, :c_local].astype(BF16)
        padded[pl.ds(edge + at * size, size), :] = total[:, c_local:] * slope[rows, :]
    grad = jnp.zeros((frames, c_local), F32)
    for tap in range(taps):
        grad = grad + taps_ref[tap : tap + 1, :] * padded[pl.ds(edge + half - tap, frames), :]
    rows = lax.broadcasted_iota(jnp.int32, (frames, c_local), 0)
    grad = jnp.where(rows < valid[0], grad, 0.0)
    gate = gate_ref[...]
    grad_value = grad * gate
    grad_gate = grad_value * value_ref[...] * (1.0 - gate)
    grad_expanded = jnp.concatenate([grad_value.astype(BF16), grad_gate.astype(BF16)], axis=1)
    for step, out in enumerate(outs):
        out[...] = dot(grad_expanded, expand_t[step], NN).astype(out.dtype)


def backward(valid, expand_t, taps, value, gate, slope, halves):
    frames, c_local = value.shape
    groups = expand_t.shape[0]
    return pl.pallas_call(
        functools.partial(backward_kernel, groups),
        out_shape=[jax.ShapeDtypeStruct((frames, c_local), BF16)]
        + [jax.ShapeDtypeStruct((frames, c_local), F32 if step == 0 else BF16) for step in range(groups)],
        in_specs=[SMEM] + [VMEM] * (5 + groups * HALVES),
        out_specs=[VMEM] * (1 + groups),
        scratch_shapes=[pltpu.VMEM((frames + 2 * edge_of(taps.shape[0]), c_local), F32)],
        compiler_params=pltpu.CompilerParams(vmem_limit_bytes=16 << 20),
        cost_estimate=matmul_cost(frames, 2 * c_local, c_local * groups),
        name="backward_module",
    )(valid, expand_t, taps, value, gate, slope, *[block for half in halves for block in half])


def partner(step, groups):
    return lax.rem(lax.axis_index("ch") + step, groups)


def swap(block, axis, count, mask):
    return lax.ppermute(block, axis, [(i, i ^ mask) for i in range(count)])


def turns(count):
    return sorted(range(1, count), key=lambda step: abs(2 * step - count))


def turn(block, count, step):
    return lax.ppermute(block, "ch", [(i, (i + step) % count) for i in range(count)])


def z_exchange(blocks):
    count = len(blocks)
    return [blocks[0]] + [turn(blocks[step], count, step) for step in turns(count)]


def z_gather(block, count, later):
    held, mask = block, count // 2
    while mask:
        arrived = swap(held, "ch", count, mask)
        if held is block:
            pass
        held = jnp.concatenate([held, arrived], axis=0)
        mask //= 2
    return held, later


def plane_exchange(blocks, count):
    return [blocks[0]] + [swap(block, "dec", count, 2 * step) for step, block in enumerate(blocks) if step]


def body(
    n_dec,
    n_ch,
    frame_cotangent,
    rollout_utterance,
    frame_offset,
    utterance_frames,
    normed_input,
    expand_weight,
    depth_kernel,
    norm_scale,
    norm_shift,
    project_weight,
    adapter_weight,
):
    u_local, frames, c_local = normed_input.shape
    width = expand_weight.shape[0]
    chips = n_dec // 2
    expand = expand_weight.reshape(width, 2 * c_local)
    taps = depth_kernel.astype(F32)
    scale, shift = norm_scale.reshape(1, c_local), norm_shift.reshape(1, c_local)

    seq_len = frame_cotangent.shape[1]
    routes = jnp.stack([rollout_utterance, frame_offset])
    for_other, own_slabs, weight = adapter_other(frames, routes, frame_cotangent, adapter_weight)
    from_other = swap(for_other, "dec", n_dec, 1)
    own = adapter_own(frames, seq_len, routes, own_slabs, weight)
    first, second = pair_sum(own, from_other)
    first, own_input = lax.optimization_barrier((first, normed_input.reshape(frames, c_local)))
    arrived = [plane_exchange(first, n_dec)]
    inputs, second = z_gather(own_input, n_ch, second)
    arrived[0], second = lax.optimization_barrier((arrived[0], second))
    arrived.append(plane_exchange(second, n_dec))
    expand_t, project_t = transposed(n_ch, expand, project_weight)
    value, gate, slope = forward(frames, utterance_frames, expand, taps, scale, shift, inputs)
    value, gate, slope, project_t = lax.optimization_barrier((value, gate, slope, project_t))
    halves = []
    for at, half in enumerate(arrived):
        halves.append(z_exchange(swish(at * frames // HALVES, utterance_frames, project_t, half)))
    stream, *parts = backward(utterance_frames, expand_t, taps, value, gate, slope, halves)
    total = sum(part.astype(F32) for part in z_exchange(parts))
    return stream[None], total.astype(BF16)[None]


def solution(mesh):
    return jax.shard_map(
        functools.partial(body, mesh.shape["dec"], mesh.shape["ch"]),
        mesh=mesh,
        in_specs=(
            P("dec", None, "ch"),
            P("dec"),
            P("dec"),
            P("dec"),
            P("dec", None, "ch"),
            P(None, None, "ch"),
            P(None, "ch"),
            P("ch"),
            P("ch"),
            P(),
            P(None, "ch"),
        ),
        out_specs=(P("dec", None, "ch"), P("dec", None, "ch")),
        check_vma=False,
    )
```

```python
import functools

import jax
import jax.numpy as jnp
from jax import lax
from jax.experimental import pallas as pl
from jax.experimental.pallas import tpu as pltpu
from jax.sharding import PartitionSpec as P

F32 = jnp.float32
BF16 = jnp.bfloat16
NT = (((1,), (1,)), ((), ()))
NN = (((1,), (0,)), ((), ()))
ROW_TILE = 16
LANES = 128
PIECES = 2
VMEM = pl.BlockSpec(memory_space=pltpu.VMEM)
SMEM = pl.BlockSpec(memory_space=pltpu.SMEM)
HBM = pl.BlockSpec(memory_space=pltpu.HBM)
HALVES = 1
OTHER_VMEM = 45
OWN_VMEM = 24
HOME_VMEM = 48


def dot(a, b, dims):
    return lax.dot_general(a, b, dims, preferred_element_type=F32)


def matmul_cost(rows, depth, columns):
    return pl.CostEstimate(
        flops=2 * rows * depth * columns,
        bytes_accessed=2 * (rows * depth + depth * columns + rows * columns),
        transcendentals=0,
    )


def picks_of(meta, flip, steps, last_start):
    dec = lax.axis_index("dec")
    picks = []
    for step in steps:
        target = ((dec // 2) ^ step) * 2 + ((dec % 2) ^ flip)
        found, first = jnp.int32(-1), jnp.int32(0)
        for roll in range(meta.shape[1]):
            hit = meta[0, roll] == target
            found = jnp.where(hit, roll, found)
            first = jnp.where(hit, meta[1, roll], first)
        start = jnp.minimum(first // ROW_TILE * ROW_TILE, last_start)
        picks.append((found, start, first - start))
    return picks


def slab_copies(windows, picks, held, sem):
    span = held.shape[0] // len(picks)
    return [
        pltpu.make_async_copy(
            windows.at[jnp.maximum(found, 0), pl.ds(pl.multiple_of(start, ROW_TILE), span), :],
            held.at[pl.ds(place * span, span), :],
            sem.at[place],
        )
        for place, (found, start, _) in enumerate(picks)
    ]


def multiply(slabs, rows, product):
    for lane in range(0, product.shape[0], 2):
        result = dot(slabs[...], rows[lane * LANES : (lane + 2) * LANES, :], NT)
        product[lane, :, :] = result[:, :LANES]
        product[lane + 1, :, :] = result[:, LANES:]


def cut_rows(product, outs, picks, first):
    frames = outs[0].shape[0]
    span = product.shape[1] // len(picks)
    for lane in range(product.shape[0]):
        for place, (found, _, shift) in enumerate(picks):
            rows = product[lane, pl.ds(place * span + shift, frames), :]
            at = first + lane * LANES
            outs[place][:, at : at + LANES] = jnp.where(found >= 0, rows, 0.0).astype(BF16)


def other_kernel(routes, windows, weight_hbm, out, own, weight, meta, slabs, *refs):
    products, (meta_sem, sem, weight_sem) = refs[:PIECES], refs[PIECES:]
    targets = out.shape[0]
    span = slabs.shape[0] // targets
    last_start = windows.shape[1] - span
    columns = weight.shape[0] // PIECES

    route_copy = pltpu.make_async_copy(routes, meta, meta_sem)
    route_copy.start()
    weights = []
    for piece in range(PIECES):
        at = pl.ds(piece * columns, columns)
        weights.append(pltpu.make_async_copy(weight_hbm.at[at, :], weight.at[at, :], weight_sem.at[piece]))
    weights[0].start()
    route_copy.wait()
    picks = picks_of(meta, 1, range(1, targets + 1), last_start)
    copies = slab_copies(windows, picks, slabs, sem.at[1])
    own_copies = slab_copies(windows, picks_of(meta, 0, range(1, targets + 1), last_start), own, sem.at[0])
    for copy in copies + weights[1:] + own_copies:
        copy.start()
    for copy in copies:
        copy.wait()
    for piece, copy in enumerate(weights):
        copy.wait()
        multiply(slabs, weight.at[pl.ds(piece * columns, columns), :], products[piece])
        cut_rows(products[piece], [out.at[place] for place in range(targets)], picks, piece * columns)
    for copy in own_copies:
        copy.wait()


def adapter_other(frames, routes, windows, weight):
    _, _, d_local = windows.shape
    width = weight.shape[0]
    targets = lax.axis_size("dec") // 2 - 1
    span = frames + ROW_TILE
    return pl.pallas_call(
        other_kernel,
        out_shape=[
            jax.ShapeDtypeStruct((targets, frames, width), BF16),
            jax.ShapeDtypeStruct((targets * span, d_local), BF16),
            jax.ShapeDtypeStruct((width, d_local), BF16),
        ],
        in_specs=[HBM] * 3,
        out_specs=[VMEM] * 3,
        scratch_shapes=[
            pltpu.SMEM(routes.shape, jnp.int32),
            pltpu.VMEM((targets * span, d_local), BF16),
        ]
        + [pltpu.VMEM((width // PIECES // LANES, targets * span, LANES), F32)] * PIECES
        + [
            pltpu.SemaphoreType.DMA,
            pltpu.SemaphoreType.DMA((2, targets)),
            pltpu.SemaphoreType.DMA((PIECES,)),
        ],
        compiler_params=pltpu.CompilerParams(vmem_limit_bytes=OTHER_VMEM << 20),
        cost_estimate=matmul_cost(targets * span, d_local, width),
        name="adapter_other",
    )(routes, windows, weight)


def own_kernel(last_start, routes, slabs, weight, out, meta, *refs):
    products, meta_sem = refs[:-1], refs[-1]
    columns = weight.shape[0] // len(products)
    route_copy = pltpu.make_async_copy(routes, meta, meta_sem)
    route_copy.start()
    multiply(slabs, weight.at[pl.ds(0, columns), :], products[0])
    route_copy.wait()
    picks = picks_of(meta, 0, range(1, out.shape[0] + 1), last_start)
    for piece, product in enumerate(products):
        if piece:
            multiply(slabs, weight.at[pl.ds(piece * columns, columns), :], product)
        cut_rows(product, [out.at[place] for place in range(out.shape[0])], picks, piece * columns)


def adapter_own(frames, seq_len, routes, slabs, weight):
    width, d_local = weight.shape
    targets = lax.axis_size("dec") // 2 - 1
    span = frames + ROW_TILE
    return pl.pallas_call(
        functools.partial(own_kernel, seq_len - span),
        out_shape=jax.ShapeDtypeStruct((targets, frames, width), BF16),
        in_specs=[HBM] + [VMEM] * 2,
        out_specs=VMEM,
        scratch_shapes=[pltpu.SMEM(routes.shape, jnp.int32)]
        + [pltpu.VMEM((width // PIECES // LANES, targets * span, LANES), F32)] * PIECES
        + [pltpu.SemaphoreType.DMA],
        compiler_params=pltpu.CompilerParams(vmem_limit_bytes=OWN_VMEM << 20),
        cost_estimate=matmul_cost(1, 1, 1),
        name="adapter_own",
    )(routes, slabs, weight)


def home_kernel(routes, windows, weight, other, own, meta, slabs, product, meta_sem, sem):
    route_copy = pltpu.make_async_copy(routes, meta, meta_sem)
    route_copy.start()
    route_copy.wait()
    last_start = windows.shape[1] - slabs.shape[0] // 2
    picks = [picks_of(meta, flip, [0], last_start)[0] for flip in (1, 0)]
    copies = slab_copies(windows, picks, slabs, sem)
    for copy in copies:
        copy.start()
    for copy in copies:
        copy.wait()
    multiply(slabs, weight, product)
    cut_rows(product, [other, own], picks, 0)


def adapter_home(frames, routes, windows, weight):
    width, d_local = weight.shape
    span = frames + ROW_TILE
    return pl.pallas_call(
        home_kernel,
        out_shape=[jax.ShapeDtypeStruct((frames, width), BF16)] * 2,
        in_specs=[HBM] * 2 + [VMEM],
        out_specs=[VMEM] * 2,
        scratch_shapes=[
            pltpu.SMEM(routes.shape, jnp.int32),
            pltpu.VMEM((2 * span, d_local), BF16),
            pltpu.VMEM((width // LANES, 2 * span, LANES), F32),
            pltpu.SemaphoreType.DMA,
            pltpu.SemaphoreType.DMA((2,)),
        ],
        compiler_params=pltpu.CompilerParams(vmem_limit_bytes=HOME_VMEM << 20),
        cost_estimate=matmul_cost(1, 1, 1),
        name="adapter_home",
    )(routes, windows, weight)


def pair_sum_kernel(own, other, *outs):
    targets, frames, _ = own.shape
    size = frames // HALVES
    for at, out in enumerate(outs):
        half, step = divmod(at, targets)
        rows = pl.ds(half * size, size)
        out[...] = (own[step, rows, :].astype(F32) + other[step, rows, :].astype(F32)).astype(BF16)


def pair_sum(own, other):
    targets, frames, width = own.shape
    outs = pl.pallas_call(
        pair_sum_kernel,
        out_shape=[jax.ShapeDtypeStruct((frames // HALVES, width), BF16)] * (targets * HALVES),
        in_specs=[VMEM] * 2,
        out_specs=[VMEM] * (targets * HALVES),
        compiler_params=pltpu.CompilerParams(vmem_limit_bytes=24 << 20),
        name="pair_sum",
    )(own, other)
    return [outs[half * targets : (half + 1) * targets] for half in range(HALVES)]


def plane_sum_kernel(*refs):
    blocks, out = refs[:-1], refs[-1]
    total = blocks[0][...].astype(F32)
    for block in blocks[1:]:
        total = total + block[...].astype(F32)
    out[...] = total


def plane_sum(blocks):
    return pl.pallas_call(
        plane_sum_kernel,
        out_shape=jax.ShapeDtypeStruct(blocks[0].shape, F32),
        in_specs=[VMEM] * len(blocks),
        out_specs=VMEM,
        compiler_params=pltpu.CompilerParams(vmem_limit_bytes=24 << 20),
        name="plane_sum",
    )(*blocks)


def swish_kernel(parts, first, valid, project, *refs):
    homes, blocks, outs, stream = refs[:2], refs[2:parts], refs[parts:-1], refs[-1]
    groups = len(outs) // 2
    frames, width = stream.shape
    c_local = outs[0].shape[1]
    total = sum(home[first : first + frames, :].astype(F32) for home in homes)
    for block in blocks:
        total = total + block[...].astype(F32)
    rows = first + lax.broadcasted_iota(jnp.int32, (frames, width), 0)
    stream[...] = jnp.where(rows < valid[0], total, 0.0).astype(BF16)
    for step in range(groups):
        at = pl.ds(pl.multiple_of(partner(step, groups) * c_local, c_local), c_local)
        outs[step][...] = dot(stream[...], project[step], NN).astype(outs[step].dtype)
        outs[groups + step][...] = stream[:, at].astype(outs[groups + step].dtype)


def swish(first, valid, project, homes, blocks):
    frames, width = blocks[0].shape
    blocks = homes + blocks
    groups, _, c_local = project.shape
    outs = pl.pallas_call(
        functools.partial(swish_kernel, len(blocks), first),
        out_shape=[jax.ShapeDtypeStruct((frames, c_local), F32 if step == 0 else BF16) for step in range(groups)] * 2,
        in_specs=[SMEM, VMEM] + [VMEM] * len(blocks),
        out_specs=[VMEM] * (2 * groups),
        scratch_shapes=[pltpu.VMEM((frames, width), BF16)],
        compiler_params=pltpu.CompilerParams(vmem_limit_bytes=24 << 20),
        cost_estimate=matmul_cost(frames, width, width),
        name="stream_and_swish",
    )(valid, project, *blocks)
    return outs[:groups], outs[groups:]


def spread_rows(padded, rows):
    frames, c_local = rows.shape
    edge = (padded.shape[0] - frames) // 2
    padded[:edge, :] = jnp.zeros((edge, c_local), F32)
    padded[edge + frames :, :] = jnp.zeros((edge, c_local), F32)
    padded[pl.ds(edge, frames), :] = rows


def edge_of(taps):
    return -(-((taps - 1) // 2) // 8) * 8


def transpose_kernel(expand, project, expand_t, project_t):
    groups, _, c_local = project_t.shape
    for step in range(groups):
        at = pl.ds(pl.multiple_of(partner(step, groups) * c_local, c_local), c_local)
        project_t[step, :, :] = project[at, :].T
        expand_t[step, :, :] = expand[at, :].T


def transposed(groups, expand, project):
    width, span = expand.shape
    c_local = width // groups
    return pl.pallas_call(
        transpose_kernel,
        out_shape=[
            jax.ShapeDtypeStruct((groups, span, c_local), BF16),
            jax.ShapeDtypeStruct((groups, width, c_local), BF16),
        ],
        in_specs=[VMEM] * 2,
        out_specs=[VMEM] * 2,
        compiler_params=pltpu.CompilerParams(vmem_limit_bytes=24 << 20),
        cost_estimate=matmul_cost(1, 1, 1),
        name="transposed_weights",
    )(expand, project)


def forward_kernel(valid, expand, taps_ref, scale, shift, inputs, value_out, gate_out, slope_out, padded):
    frames, c_local = value_out.shape
    taps = taps_ref.shape[0]
    half = (taps - 1) // 2
    edge = (padded.shape[0] - frames) // 2
    expanded = jnp.zeros((frames, 2 * c_local), F32)
    masks = [0]
    while len(masks) * frames < inputs.shape[0]:
        far = inputs.shape[0] // frames // 2 // len(masks)
        masks += [mask ^ far for mask in masks]
    for place, mask in enumerate(masks):
        at = pl.ds(pl.multiple_of((lax.axis_index("ch") ^ mask) * c_local, c_local), c_local)
        expanded = expanded + dot(inputs[place * frames : (place + 1) * frames, :], expand[at, :], NN)
    value = expanded[:, :c_local]
    gate = jax.nn.sigmoid(expanded[:, c_local:])
    rows = lax.broadcasted_iota(jnp.int32, (frames, c_local), 0)
    spread_rows(padded, jnp.where(rows < valid[0], value * gate, 0.0))
    depth = jnp.zeros((frames, c_local), F32)
    for tap in range(taps):
        depth = depth + taps_ref[tap : tap + 1, :] * padded[pl.ds(edge - half + tap, frames), :]
    shifted = depth * scale[...] + shift[...]
    sig = jax.nn.sigmoid(shifted)
    value_out[...] = value
    gate_out[...] = gate
    slope_out[...] = sig * (1.0 + shifted * (1.0 - sig)) * scale[...]


def forward(frames, valid, expand, taps, scale, shift, inputs):
    width, c_local = expand.shape[0], inputs.shape[1]
    return pl.pallas_call(
        forward_kernel,
        out_shape=[jax.ShapeDtypeStruct((frames, c_local), F32)] * 3,
        in_specs=[SMEM] + [VMEM] * 5,
        out_specs=[VMEM] * 3,
        scratch_shapes=[pltpu.VMEM((frames + 2 * edge_of(taps.shape[0]), c_local), F32)],
        compiler_params=pltpu.CompilerParams(vmem_limit_bytes=24 << 20),
        cost_estimate=matmul_cost(frames, width, 2 * c_local),
        name="forward_gates",
    )(valid, expand, taps, scale, shift, inputs)


def backward_kernel(parts, valid, expand_t, taps_ref, value_ref, gate_ref, slope, *refs):
    blocks, outs, padded = refs[:parts], refs[parts:-1], refs[-1]
    frames, c_local = value_ref.shape
    taps = taps_ref.shape[0]
    half = (taps - 1) // 2
    edge = (padded.shape[0] - frames) // 2
    total = blocks[0][...].astype(F32)
    for block in blocks[1:]:
        total = total + block[...].astype(F32)
    spread_rows(padded, total * slope[...])
    grad = jnp.zeros((frames, c_local), F32)
    for tap in range(taps):
        grad = grad + taps_ref[tap : tap + 1, :] * padded[pl.ds(edge + half - tap, frames), :]
    rows = lax.broadcasted_iota(jnp.int32, (frames, c_local), 0)
    grad = jnp.where(rows < valid[0], grad, 0.0)
    gate = gate_ref[...]
    grad_value = grad * gate
    grad_gate = grad_value * value_ref[...] * (1.0 - gate)
    grad_expanded = jnp.concatenate([grad_value.astype(BF16), grad_gate.astype(BF16)], axis=1)
    for step, out in enumerate(outs):
        out[...] = dot(grad_expanded, expand_t[step], NN).astype(out.dtype)


def backward(valid, expand_t, taps, value, gate, slope, blocks):
    frames, c_local = value.shape
    groups = expand_t.shape[0]
    return pl.pallas_call(
        functools.partial(backward_kernel, groups),
        out_shape=[jax.ShapeDtypeStruct((frames, c_local), F32 if step == 0 else BF16) for step in range(groups)],
        in_specs=[SMEM] + [VMEM] * (5 + groups),
        out_specs=[VMEM] * groups,
        scratch_shapes=[pltpu.VMEM((frames + 2 * edge_of(taps.shape[0]), c_local), F32)],
        compiler_params=pltpu.CompilerParams(vmem_limit_bytes=16 << 20),
        cost_estimate=matmul_cost(frames, 2 * c_local, c_local * groups),
        name="backward_module",
    )(valid, expand_t, taps, value, gate, slope, *blocks)


def partner(step, groups):
    return lax.rem(lax.axis_index("ch") + step, groups)


def swap(block, axis, count, mask):
    return lax.ppermute(block, axis, [(i, i ^ mask) for i in range(count)])


def turns(count):
    return sorted(range(1, count), key=lambda step: abs(2 * step - count))


def turn(block, count, step):
    return lax.ppermute(block, "ch", [(i, (i + step) % count) for i in range(count)])


def z_exchange(blocks):
    count = len(blocks)
    return [blocks[0]] + [turn(blocks[step], count, step) for step in turns(count)]


def z_gather(block, count, later):
    held, mask = block, count // 2
    while mask:
        arrived = swap(held, "ch", count, mask)
        held = jnp.concatenate([held, arrived], axis=0)
        mask //= 2
    return held, later


def summed(blocks):
    return sum(block.astype(F32) for block in blocks).astype(BF16)


def plane_exchange(blocks, count):
    return [swap(block, "dec", count, 2 * step) for step, block in enumerate(blocks, 1)]


def body(
    n_dec,
    n_ch,
    frame_cotangent,
    rollout_utterance,
    frame_offset,
    utterance_frames,
    normed_input,
    expand_weight,
    depth_kernel,
    norm_scale,
    norm_shift,
    project_weight,
    adapter_weight,
):
    u_local, frames, c_local = normed_input.shape
    width = expand_weight.shape[0]
    chips = n_dec // 2
    expand = expand_weight.reshape(width, 2 * c_local)
    taps = depth_kernel.astype(F32)
    scale, shift = norm_scale.reshape(1, c_local), norm_shift.reshape(1, c_local)

    seq_len = frame_cotangent.shape[1]
    routes = jnp.stack([rollout_utterance, frame_offset])
    for_other, own_slabs, weight = adapter_other(frames, routes, frame_cotangent, adapter_weight)
    from_other = swap(for_other, "dec", n_dec, 1)
    own = adapter_own(frames, seq_len, routes, own_slabs, weight)
    (sums,) = pair_sum(own, from_other)
    sums, routes, own_input = lax.optimization_barrier((sums, routes, normed_input.reshape(frames, c_local)))
    arrived = plane_exchange(sums, n_dec)
    home_other, home_own = adapter_home(frames, routes, frame_cotangent, weight)
    homes = [home_own, swap(home_other, "dec", n_dec, 1)]
    inputs, _ = z_gather(own_input, n_ch, taps)
    expand_t, project_t = transposed(n_ch, expand, project_weight)
    value, gate, slope = forward(frames, utterance_frames, expand, taps, scale, shift, inputs)
    swish_parts, stream_parts = swish(0, utterance_frames, project_t, homes, [plane_sum(arrived)])
    swish_parts = z_exchange(swish_parts)
    stream_parts = z_exchange(stream_parts)
    parts = z_exchange(backward(utterance_frames, expand_t, taps, value, gate, slope, swish_parts))
    return summed(stream_parts)[None], summed(parts)[None]


def solution(mesh):
    return jax.shard_map(
        functools.partial(body, mesh.shape["dec"], mesh.shape["ch"]),
        mesh=mesh,
        in_specs=(
            P("dec", None, "ch"),
            P("dec"),
            P("dec"),
            P("dec"),
            P("dec", None, "ch"),
            P(None, None, "ch"),
            P(None, "ch"),
            P("ch"),
            P("ch"),
            P(),
            P(None, "ch"),
        ),
        out_specs=(P("dec", None, "ch"), P("dec", None, "ch")),
        check_vma=False,
    )
```

```python
import functools

import jax
import jax.numpy as jnp
from jax import lax
from jax.experimental import pallas as pl
from jax.experimental.pallas import tpu as pltpu
from jax.sharding import PartitionSpec as P

F32 = jnp.float32
BF16 = jnp.bfloat16
NT = (((1,), (1,)), ((), ()))
NN = (((1,), (0,)), ((), ()))
ROW_TILE = 16
LANES = 128
PIECES = 2
VMEM = pl.BlockSpec(memory_space=pltpu.VMEM)
SMEM = pl.BlockSpec(memory_space=pltpu.SMEM)
HBM = pl.BlockSpec(memory_space=pltpu.HBM)
HALVES = 1
OTHER_VMEM = 45
OWN_VMEM = 24


def dot(a, b, dims):
    return lax.dot_general(a, b, dims, preferred_element_type=F32)


def matmul_cost(rows, depth, columns):
    return pl.CostEstimate(
        flops=2 * rows * depth * columns,
        bytes_accessed=2 * (rows * depth + depth * columns + rows * columns),
        transcendentals=0,
    )


def picks_of(meta, flip, steps, last_start):
    dec = lax.axis_index("dec")
    picks = []
    for step in steps:
        target = ((dec // 2) ^ step) * 2 + ((dec % 2) ^ flip)
        found, first = jnp.int32(-1), jnp.int32(0)
        for roll in range(meta.shape[1]):
            hit = meta[0, roll] == target
            found = jnp.where(hit, roll, found)
            first = jnp.where(hit, meta[1, roll], first)
        start = jnp.minimum(first // ROW_TILE * ROW_TILE, last_start)
        picks.append((found, start, first - start))
    return picks


def slab_copies(windows, picks, held, sem):
    span = held.shape[0] // len(picks)
    return [
        pltpu.make_async_copy(
            windows.at[jnp.maximum(found, 0), pl.ds(pl.multiple_of(start, ROW_TILE), span), :],
            held.at[pl.ds(place * span, span), :],
            sem.at[place],
        )
        for place, (found, start, _) in enumerate(picks)
    ]


def multiply(slabs, rows, product):
    for lane in range(0, product.shape[0], 2):
        result = dot(slabs[...], rows[lane * LANES : (lane + 2) * LANES, :], NT)
        product[lane, :, :] = result[:, :LANES]
        product[lane + 1, :, :] = result[:, LANES:]


def cut_rows(product, outs, picks, first):
    frames = outs[0].shape[0]
    span = product.shape[1] // len(picks)
    for lane in range(product.shape[0]):
        for place, (found, _, shift) in enumerate(picks):
            rows = product[lane, pl.ds(place * span + shift, frames), :]
            at = first + lane * LANES
            outs[place][:, at : at + LANES] = jnp.where(found >= 0, rows, 0.0).astype(BF16)


def other_kernel(routes, windows, weight_hbm, out, own, home, weight, meta, slabs, *refs):
    products, (meta_sem, sem, weight_sem) = refs[:PIECES], refs[PIECES:]
    targets = out.shape[0]
    span = slabs.shape[0] // targets
    last_start = windows.shape[1] - span
    columns = weight.shape[0] // PIECES

    route_copy = pltpu.make_async_copy(routes, meta, meta_sem)
    route_copy.start()
    weights = []
    for piece in range(PIECES):
        at = pl.ds(piece * columns, columns)
        weights.append(pltpu.make_async_copy(weight_hbm.at[at, :], weight.at[at, :], weight_sem.at[piece]))
    weights[0].start()
    route_copy.wait()
    picks = picks_of(meta, 1, range(1, targets + 1), last_start)
    copies = slab_copies(windows, picks, slabs, sem.at[1])
    own_copies = slab_copies(windows, picks_of(meta, 0, range(1, targets + 1), last_start), own, sem.at[0])
    home_picks = [picks_of(meta, flip, [0], last_start)[0] for flip in (1, 0)]
    own_copies += slab_copies(windows, home_picks, home, sem.at[2])
    for copy in copies + weights[1:] + own_copies:
        copy.start()
    for copy in copies:
        copy.wait()
    for piece, copy in enumerate(weights):
        copy.wait()
        multiply(slabs, weight.at[pl.ds(piece * columns, columns), :], products[piece])
        cut_rows(products[piece], [out.at[place] for place in range(targets)], picks, piece * columns)
    for copy in own_copies:
        copy.wait()


def adapter_other(frames, routes, windows, weight):
    _, _, d_local = windows.shape
    width = weight.shape[0]
    targets = lax.axis_size("dec") // 2 - 1
    span = frames + ROW_TILE
    return pl.pallas_call(
        other_kernel,
        out_shape=[
            jax.ShapeDtypeStruct((targets, frames, width), BF16),
            jax.ShapeDtypeStruct((targets * span, d_local), BF16),
            jax.ShapeDtypeStruct((2 * span, d_local), BF16),
            jax.ShapeDtypeStruct((width, d_local), BF16),
        ],
        in_specs=[HBM] * 3,
        out_specs=[VMEM] * 4,
        scratch_shapes=[
            pltpu.SMEM(routes.shape, jnp.int32),
            pltpu.VMEM((targets * span, d_local), BF16),
        ]
        + [pltpu.VMEM((width // PIECES // LANES, targets * span, LANES), F32)] * PIECES
        + [
            pltpu.SemaphoreType.DMA,
            pltpu.SemaphoreType.DMA((3, max(targets, 2))),
            pltpu.SemaphoreType.DMA((PIECES,)),
        ],
        compiler_params=pltpu.CompilerParams(vmem_limit_bytes=OTHER_VMEM << 20),
        cost_estimate=matmul_cost(targets * span, d_local, width),
        name="adapter_other",
    )(routes, windows, weight)


def own_kernel(last_start, routes, slabs, weight, out, meta, *refs):
    products, meta_sem = refs[:-1], refs[-1]
    columns = weight.shape[0] // len(products)
    route_copy = pltpu.make_async_copy(routes, meta, meta_sem)
    route_copy.start()
    multiply(slabs, weight.at[pl.ds(0, columns), :], products[0])
    route_copy.wait()
    picks = picks_of(meta, 0, range(1, out.shape[0] + 1), last_start)
    for piece, product in enumerate(products):
        if piece:
            multiply(slabs, weight.at[pl.ds(piece * columns, columns), :], product)
        cut_rows(product, [out.at[place] for place in range(out.shape[0])], picks, piece * columns)


def adapter_own(frames, seq_len, routes, slabs, weight):
    width, d_local = weight.shape
    targets = lax.axis_size("dec") // 2 - 1
    span = frames + ROW_TILE
    return pl.pallas_call(
        functools.partial(own_kernel, seq_len - span),
        out_shape=jax.ShapeDtypeStruct((targets, frames, width), BF16),
        in_specs=[HBM] + [VMEM] * 2,
        out_specs=VMEM,
        scratch_shapes=[pltpu.SMEM(routes.shape, jnp.int32)]
        + [pltpu.VMEM((width // PIECES // LANES, targets * span, LANES), F32)] * PIECES
        + [pltpu.SemaphoreType.DMA],
        compiler_params=pltpu.CompilerParams(vmem_limit_bytes=OWN_VMEM << 20),
        cost_estimate=matmul_cost(1, 1, 1),
        name="adapter_own",
    )(routes, slabs, weight)


def home_kernel(last_start, routes, slabs, weight, other, own, meta, product, meta_sem):
    route_copy = pltpu.make_async_copy(routes, meta, meta_sem)
    route_copy.start()
    multiply(slabs, weight, product)
    route_copy.wait()
    picks = [picks_of(meta, flip, [0], last_start)[0] for flip in (1, 0)]
    cut_rows(product, [other, own], picks, 0)


def adapter_home(frames, seq_len, routes, slabs, weight):
    width = weight.shape[0]
    span = frames + ROW_TILE
    return pl.pallas_call(
        functools.partial(home_kernel, seq_len - span),
        out_shape=[jax.ShapeDtypeStruct((frames, width), BF16)] * 2,
        in_specs=[HBM] + [VMEM] * 2,
        out_specs=[VMEM] * 2,
        scratch_shapes=[
            pltpu.SMEM(routes.shape, jnp.int32),
            pltpu.VMEM((width // LANES, 2 * span, LANES), F32),
            pltpu.SemaphoreType.DMA,
        ],
        compiler_params=pltpu.CompilerParams(vmem_limit_bytes=OWN_VMEM << 20),
        cost_estimate=matmul_cost(1, 1, 1),
        name="adapter_home",
    )(routes, slabs, weight)


def pair_sum_kernel(own, other, *outs):
    targets, frames, _ = own.shape
    size = frames // HALVES
    for at, out in enumerate(outs):
        half, step = divmod(at, targets)
        rows = pl.ds(half * size, size)
        out[...] = (own[step, rows, :].astype(F32) + other[step, rows, :].astype(F32)).astype(BF16)


def pair_sum(own, other):
    targets, frames, width = own.shape
    outs = pl.pallas_call(
        pair_sum_kernel,
        out_shape=[jax.ShapeDtypeStruct((frames // HALVES, width), BF16)] * (targets * HALVES),
        in_specs=[VMEM] * 2,
        out_specs=[VMEM] * (targets * HALVES),
        compiler_params=pltpu.CompilerParams(vmem_limit_bytes=24 << 20),
        name="pair_sum",
    )(own, other)
    return [outs[half * targets : (half + 1) * targets] for half in range(HALVES)]


def plane_sum_kernel(*refs):
    blocks, out = refs[:-1], refs[-1]
    total = blocks[0][...].astype(F32)
    for block in blocks[1:]:
        total = total + block[...].astype(F32)
    out[...] = total


def plane_sum(blocks):
    return pl.pallas_call(
        plane_sum_kernel,
        out_shape=jax.ShapeDtypeStruct(blocks[0].shape, F32),
        in_specs=[VMEM] * len(blocks),
        out_specs=VMEM,
        compiler_params=pltpu.CompilerParams(vmem_limit_bytes=24 << 20),
        name="plane_sum",
    )(*blocks)


def square_sum_kernel(own, other, along_x, along_y, keep_x, keep_y):
    size = keep_x.shape[0]
    first, second = pl.ds(0, size), pl.ds(size, size)

    def both(place, rows):
        return (own[place, rows, :].astype(F32) + other[place, rows, :].astype(F32)).astype(BF16)

    along_x[0, :, :] = both(0, first)
    along_x[1, :, :] = both(2, first)
    along_y[0, :, :] = both(1, second)
    along_y[1, :, :] = both(2, second)
    keep_x[...] = both(1, first)
    keep_y[...] = both(0, second)


def square_sum(own, other):
    _, frames, width = own.shape
    pair = jax.ShapeDtypeStruct((2, frames // 2, width), BF16)
    single = jax.ShapeDtypeStruct((frames // 2, width), BF16)
    return pl.pallas_call(
        square_sum_kernel,
        out_shape=[pair, pair, single, single],
        in_specs=[VMEM] * 2,
        out_specs=[VMEM] * 4,
        compiler_params=pltpu.CompilerParams(vmem_limit_bytes=24 << 20),
        name="pair_sum",
    )(own, other)


def relay_kernel(keep, arrived, out):
    out[...] = (keep[...].astype(F32) + arrived[1].astype(F32)).astype(BF16)


def relay(keep, arrived):
    return pl.pallas_call(
        relay_kernel,
        out_shape=jax.ShapeDtypeStruct(keep.shape, BF16),
        in_specs=[VMEM] * 2,
        out_specs=VMEM,
        compiler_params=pltpu.CompilerParams(vmem_limit_bytes=24 << 20),
        name="relay",
    )(keep, arrived)


def square_total_kernel(from_x, relayed_x, from_y, relayed_y, out):
    size = relayed_x.shape[0]
    out[:size, :] = from_x[0].astype(F32) + relayed_x[...].astype(F32)
    out[size:, :] = from_y[0].astype(F32) + relayed_y[...].astype(F32)


def square_total(from_x, relayed_x, from_y, relayed_y):
    size, width = relayed_x.shape
    return pl.pallas_call(
        square_total_kernel,
        out_shape=jax.ShapeDtypeStruct((2 * size, width), F32),
        in_specs=[VMEM] * 4,
        out_specs=VMEM,
        compiler_params=pltpu.CompilerParams(vmem_limit_bytes=24 << 20),
        name="plane_sum",
    )(from_x, relayed_x, from_y, relayed_y)


def swish_kernel(parts, first, valid, project, *refs):
    homes, blocks, outs, stream = refs[:2], refs[2:parts], refs[parts:-1], refs[-1]
    groups = len(outs) // 2
    frames, width = stream.shape
    c_local = outs[0].shape[1]
    total = sum(home[first : first + frames, :].astype(F32) for home in homes)
    for block in blocks:
        total = total + block[...].astype(F32)
    rows = first + lax.broadcasted_iota(jnp.int32, (frames, width), 0)
    stream[...] = jnp.where(rows < valid[0], total, 0.0).astype(BF16)
    for step in range(groups):
        at = pl.ds(pl.multiple_of(partner(step, groups) * c_local, c_local), c_local)
        outs[step][...] = dot(stream[...], project[step], NN).astype(outs[step].dtype)
        outs[groups + step][...] = stream[:, at].astype(outs[groups + step].dtype)


def swish(first, valid, project, homes, blocks):
    frames, width = blocks[0].shape
    blocks = homes + blocks
    groups, _, c_local = project.shape
    outs = pl.pallas_call(
        functools.partial(swish_kernel, len(blocks), first),
        out_shape=[jax.ShapeDtypeStruct((frames, c_local), F32 if step == 0 else BF16) for step in range(groups)] * 2,
        in_specs=[SMEM, VMEM] + [VMEM] * len(blocks),
        out_specs=[VMEM] * (2 * groups),
        scratch_shapes=[pltpu.VMEM((frames, width), BF16)],
        compiler_params=pltpu.CompilerParams(vmem_limit_bytes=24 << 20),
        cost_estimate=matmul_cost(frames, width, width),
        name="stream_and_swish",
    )(valid, project, *blocks)
    return outs[:groups], outs[groups:]


def spread_rows(padded, rows):
    frames, c_local = rows.shape
    edge = (padded.shape[0] - frames) // 2
    padded[:edge, :] = jnp.zeros((edge, c_local), F32)
    padded[edge + frames :, :] = jnp.zeros((edge, c_local), F32)
    padded[pl.ds(edge, frames), :] = rows


def edge_of(taps):
    return -(-((taps - 1) // 2) // 8) * 8


def transpose_kernel(expand, project, expand_t, project_t):
    groups, _, c_local = project_t.shape
    for step in range(groups):
        at = pl.ds(pl.multiple_of(partner(step, groups) * c_local, c_local), c_local)
        project_t[step, :, :] = project[at, :].T
        expand_t[step, :, :] = expand[at, :].T


def transposed(groups, expand, project):
    width, span = expand.shape
    c_local = width // groups
    return pl.pallas_call(
        transpose_kernel,
        out_shape=[
            jax.ShapeDtypeStruct((groups, span, c_local), BF16),
            jax.ShapeDtypeStruct((groups, width, c_local), BF16),
        ],
        in_specs=[VMEM] * 2,
        out_specs=[VMEM] * 2,
        compiler_params=pltpu.CompilerParams(vmem_limit_bytes=24 << 20),
        cost_estimate=matmul_cost(1, 1, 1),
        name="transposed_weights",
    )(expand, project)


def forward_kernel(valid, expand, taps_ref, scale, shift, inputs, value_out, gate_out, slope_out, padded):
    frames, c_local = value_out.shape
    taps = taps_ref.shape[0]
    half = (taps - 1) // 2
    edge = (padded.shape[0] - frames) // 2
    expanded = jnp.zeros((frames, 2 * c_local), F32)
    masks = [0]
    while len(masks) * frames < inputs.shape[0]:
        far = inputs.shape[0] // frames // 2 // len(masks)
        masks += [mask ^ far for mask in masks]
    for place, mask in enumerate(masks):
        at = pl.ds(pl.multiple_of((lax.axis_index("ch") ^ mask) * c_local, c_local), c_local)
        expanded = expanded + dot(inputs[place * frames : (place + 1) * frames, :], expand[at, :], NN)
    value = expanded[:, :c_local]
    gate = jax.nn.sigmoid(expanded[:, c_local:])
    rows = lax.broadcasted_iota(jnp.int32, (frames, c_local), 0)
    spread_rows(padded, jnp.where(rows < valid[0], value * gate, 0.0))
    depth = jnp.zeros((frames, c_local), F32)
    for tap in range(taps):
        depth = depth + taps_ref[tap : tap + 1, :] * padded[pl.ds(edge - half + tap, frames), :]
    shifted = depth * scale[...] + shift[...]
    sig = jax.nn.sigmoid(shifted)
    value_out[...] = value
    gate_out[...] = gate
    slope_out[...] = sig * (1.0 + shifted * (1.0 - sig)) * scale[...]


def forward(frames, valid, expand, taps, scale, shift, inputs):
    width, c_local = expand.shape[0], inputs.shape[1]
    return pl.pallas_call(
        forward_kernel,
        out_shape=[jax.ShapeDtypeStruct((frames, c_local), F32)] * 3,
        in_specs=[SMEM] + [VMEM] * 5,
        out_specs=[VMEM] * 3,
        scratch_shapes=[pltpu.VMEM((frames + 2 * edge_of(taps.shape[0]), c_local), F32)],
        compiler_params=pltpu.CompilerParams(vmem_limit_bytes=24 << 20),
        cost_estimate=matmul_cost(frames, width, 2 * c_local),
        name="forward_gates",
    )(valid, expand, taps, scale, shift, inputs)


def backward_kernel(parts, valid, expand_t, taps_ref, value_ref, gate_ref, slope, *refs):
    blocks, outs, padded = refs[:parts], refs[parts:-1], refs[-1]
    frames, c_local = value_ref.shape
    taps = taps_ref.shape[0]
    half = (taps - 1) // 2
    edge = (padded.shape[0] - frames) // 2
    total = blocks[0][...].astype(F32)
    for block in blocks[1:]:
        total = total + block[...].astype(F32)
    spread_rows(padded, total * slope[...])
    grad = jnp.zeros((frames, c_local), F32)
    for tap in range(taps):
        grad = grad + taps_ref[tap : tap + 1, :] * padded[pl.ds(edge + half - tap, frames), :]
    rows = lax.broadcasted_iota(jnp.int32, (frames, c_local), 0)
    grad = jnp.where(rows < valid[0], grad, 0.0)
    gate = gate_ref[...]
    grad_value = grad * gate
    grad_gate = grad_value * value_ref[...] * (1.0 - gate)
    grad_expanded = jnp.concatenate([grad_value.astype(BF16), grad_gate.astype(BF16)], axis=1)
    for step, out in enumerate(outs):
        out[...] = dot(grad_expanded, expand_t[step], NN).astype(out.dtype)


def backward(valid, expand_t, taps, value, gate, slope, blocks):
    frames, c_local = value.shape
    groups = expand_t.shape[0]
    return pl.pallas_call(
        functools.partial(backward_kernel, groups),
        out_shape=[jax.ShapeDtypeStruct((frames, c_local), F32 if step == 0 else BF16) for step in range(groups)],
        in_specs=[SMEM] + [VMEM] * (5 + groups),
        out_specs=[VMEM] * groups,
        scratch_shapes=[pltpu.VMEM((frames + 2 * edge_of(taps.shape[0]), c_local), F32)],
        compiler_params=pltpu.CompilerParams(vmem_limit_bytes=16 << 20),
        cost_estimate=matmul_cost(frames, 2 * c_local, c_local * groups),
        name="backward_module",
    )(valid, expand_t, taps, value, gate, slope, *blocks)


def partner(step, groups):
    return lax.rem(lax.axis_index("ch") + step, groups)


def swap(block, axis, count, mask):
    return lax.ppermute(block, axis, [(i, i ^ mask) for i in range(count)])


def turns(count):
    return sorted(range(1, count), key=lambda step: abs(2 * step - count))


def turn(block, count, step):
    return lax.ppermute(block, "ch", [(i, (i + step) % count) for i in range(count)])


def z_exchange(blocks):
    count = len(blocks)
    return [blocks[0]] + [turn(blocks[step], count, step) for step in turns(count)]


def z_gather(block, count):
    held, mask = block, count // 2
    while mask:
        arrived = swap(held, "ch", count, mask)
        held = jnp.concatenate([held, arrived], axis=0)
        mask //= 2
    return held


def summed(blocks):
    return sum(block.astype(F32) for block in blocks).astype(BF16)


def plane_exchange(blocks, count):
    return [swap(block, "dec", count, 2 * step) for step, block in enumerate(blocks, 1)]


def body(
    n_dec,
    n_ch,
    frame_cotangent,
    rollout_utterance,
    frame_offset,
    utterance_frames,
    normed_input,
    expand_weight,
    depth_kernel,
    norm_scale,
    norm_shift,
    project_weight,
    adapter_weight,
):
    u_local, frames, c_local = normed_input.shape
    width = expand_weight.shape[0]
    chips = n_dec // 2
    expand = expand_weight.reshape(width, 2 * c_local)
    taps = depth_kernel.astype(F32)
    scale, shift = norm_scale.reshape(1, c_local), norm_shift.reshape(1, c_local)

    seq_len = frame_cotangent.shape[1]
    routes = jnp.stack([rollout_utterance, frame_offset])
    for_other, own_slabs, home_slabs, weight = adapter_other(frames, routes, frame_cotangent, adapter_weight)
    from_other = swap(for_other, "dec", n_dec, 1)
    own = adapter_own(frames, seq_len, routes, own_slabs, weight)
    square = chips == 4
    sums = square_sum(own, from_other) if square else pair_sum(own, from_other)[0]
    sums, routes, own_input = lax.optimization_barrier((sums, routes, normed_input.reshape(frames, c_local)))
    if square:
        from_x, from_y = swap(sums[0], "dec", n_dec, 2), swap(sums[1], "dec", n_dec, 4)
        relayed_x = swap(relay(sums[2], from_x), "dec", n_dec, 4)
        relayed_y = swap(relay(sums[3], from_y), "dec", n_dec, 2)
        arrived = square_total(from_x, relayed_x, from_y, relayed_y)
    else:
        arrived = plane_sum(plane_exchange(sums, n_dec))
    home_other, home_own = adapter_home(frames, seq_len, routes, home_slabs, weight)
    homes = [home_own, swap(home_other, "dec", n_dec, 1)]
    inputs = z_gather(own_input, n_ch)
    expand_t, project_t = transposed(n_ch, expand, project_weight)
    value, gate, slope = forward(frames, utterance_frames, expand, taps, scale, shift, inputs)
    swish_parts, stream_parts = swish(0, utterance_frames, project_t, homes, [arrived])
    swish_parts = z_exchange(swish_parts)
    stream_parts = z_exchange(stream_parts)
    parts = z_exchange(backward(utterance_frames, expand_t, taps, value, gate, slope, swish_parts))
    return summed(stream_parts)[None], summed(parts)[None]


def solution(mesh):
    return jax.shard_map(
        functools.partial(body, mesh.shape["dec"], mesh.shape["ch"]),
        mesh=mesh,
        in_specs=(
            P("dec", None, "ch"),
            P("dec"),
            P("dec"),
            P("dec"),
            P("dec", None, "ch"),
            P(None, None, "ch"),
            P(None, "ch"),
            P("ch"),
            P("ch"),
            P(),
            P(None, "ch"),
        ),
        out_specs=(P("dec", None, "ch"), P("dec", None, "ch")),
        check_vma=False,
    )
```

```python
import functools

import jax
import jax.numpy as jnp
from jax import lax
from jax.experimental import pallas as pl
from jax.experimental.pallas import tpu as pltpu
from jax.sharding import PartitionSpec as P

F32 = jnp.float32
BF16 = jnp.bfloat16
NT = (((1,), (1,)), ((), ()))
NN = (((1,), (0,)), ((), ()))
ROW_TILE = 16
LANES = 128
PIECES = 2
VMEM = pl.BlockSpec(memory_space=pltpu.VMEM)
SMEM = pl.BlockSpec(memory_space=pltpu.SMEM)
HBM = pl.BlockSpec(memory_space=pltpu.HBM)
HALVES = 1
OTHER_VMEM = 45
OWN_VMEM = 24


def dot(a, b, dims):
    return lax.dot_general(a, b, dims, preferred_element_type=F32)


def matmul_cost(rows, depth, columns):
    return pl.CostEstimate(
        flops=2 * rows * depth * columns,
        bytes_accessed=2 * (rows * depth + depth * columns + rows * columns),
        transcendentals=0,
    )


def picks_of(meta, flip, steps, last_start):
    dec = lax.axis_index("dec")
    picks = []
    for step in steps:
        target = ((dec // 2) ^ step) * 2 + ((dec % 2) ^ flip)
        found, first = jnp.int32(-1), jnp.int32(0)
        for roll in range(meta.shape[1]):
            hit = meta[0, roll] == target
            found = jnp.where(hit, roll, found)
            first = jnp.where(hit, meta[1, roll], first)
        start = jnp.minimum(first // ROW_TILE * ROW_TILE, last_start)
        picks.append((found, start, first - start))
    return picks


def slab_copies(windows, picks, held, sem):
    span = held.shape[0] // len(picks)
    return [
        pltpu.make_async_copy(
            windows.at[jnp.maximum(found, 0), pl.ds(pl.multiple_of(start, ROW_TILE), span), :],
            held.at[pl.ds(place * span, span), :],
            sem.at[place],
        )
        for place, (found, start, _) in enumerate(picks)
    ]


def multiply(slabs, rows, product):
    for lane in range(0, product.shape[0], 2):
        result = dot(slabs[...], rows[lane * LANES : (lane + 2) * LANES, :], NT)
        product[lane, :, :] = result[:, :LANES]
        product[lane + 1, :, :] = result[:, LANES:]


def cut_rows(product, outs, picks, first):
    frames = outs[0].shape[0]
    span = product.shape[1] // len(picks)
    for lane in range(product.shape[0]):
        for place, (found, _, shift) in enumerate(picks):
            rows = product[lane, pl.ds(place * span + shift, frames), :]
            at = first + lane * LANES
            outs[place][:, at : at + LANES] = jnp.where(found >= 0, rows, 0.0).astype(BF16)


def other_kernel(routes, windows, weight_hbm, out, own, home, weight, meta, slabs, *refs):
    products, (meta_sem, sem, weight_sem) = refs[:PIECES], refs[PIECES:]
    targets = out.shape[0]
    span = slabs.shape[0] // targets
    last_start = windows.shape[1] - span
    columns = weight.shape[0] // PIECES

    route_copy = pltpu.make_async_copy(routes, meta, meta_sem)
    route_copy.start()
    weights = []
    for piece in range(PIECES):
        at = pl.ds(piece * columns, columns)
        weights.append(pltpu.make_async_copy(weight_hbm.at[at, :], weight.at[at, :], weight_sem.at[piece]))
    weights[0].start()
    route_copy.wait()
    picks = picks_of(meta, 1, range(1, targets + 1), last_start)
    copies = slab_copies(windows, picks, slabs, sem.at[1])
    own_copies = slab_copies(windows, picks_of(meta, 0, range(1, targets + 1), last_start), own, sem.at[0])
    home_picks = [picks_of(meta, flip, [0], last_start)[0] for flip in (1, 0)]
    own_copies += slab_copies(windows, home_picks, home, sem.at[2])
    for copy in copies + weights[1:] + own_copies:
        copy.start()
    for copy in copies:
        copy.wait()
    for piece, copy in enumerate(weights):
        copy.wait()
        multiply(slabs, weight.at[pl.ds(piece * columns, columns), :], products[piece])
        cut_rows(products[piece], [out.at[place] for place in range(targets)], picks, piece * columns)
    for copy in own_copies:
        copy.wait()


def adapter_other(frames, routes, windows, weight):
    _, _, d_local = windows.shape
    width = weight.shape[0]
    targets = lax.axis_size("dec") // 2 - 1
    span = frames + ROW_TILE
    return pl.pallas_call(
        other_kernel,
        out_shape=[
            jax.ShapeDtypeStruct((targets, frames, width), BF16),
            jax.ShapeDtypeStruct((targets * span, d_local), BF16),
            jax.ShapeDtypeStruct((2 * span, d_local), BF16),
            jax.ShapeDtypeStruct((width, d_local), BF16),
        ],
        in_specs=[HBM] * 3,
        out_specs=[VMEM] * 4,
        scratch_shapes=[
            pltpu.SMEM(routes.shape, jnp.int32),
            pltpu.VMEM((targets * span, d_local), BF16),
        ]
        + [pltpu.VMEM((width // PIECES // LANES, targets * span, LANES), F32)] * PIECES
        + [
            pltpu.SemaphoreType.DMA,
            pltpu.SemaphoreType.DMA((3, max(targets, 2))),
            pltpu.SemaphoreType.DMA((PIECES,)),
        ],
        compiler_params=pltpu.CompilerParams(vmem_limit_bytes=OTHER_VMEM << 20),
        cost_estimate=matmul_cost(targets * span, d_local, width),
        name="adapter_other",
    )(routes, windows, weight)


def own_kernel(last_start, routes, slabs, weight, out, meta, *refs):
    products, meta_sem = refs[:-1], refs[-1]
    columns = weight.shape[0] // len(products)
    route_copy = pltpu.make_async_copy(routes, meta, meta_sem)
    route_copy.start()
    multiply(slabs, weight.at[pl.ds(0, columns), :], products[0])
    route_copy.wait()
    picks = picks_of(meta, 0, range(1, out.shape[0] + 1), last_start)
    for piece, product in enumerate(products):
        if piece:
            multiply(slabs, weight.at[pl.ds(piece * columns, columns), :], product)
        cut_rows(product, [out.at[place] for place in range(out.shape[0])], picks, piece * columns)


def adapter_own(frames, seq_len, routes, slabs, weight):
    width, d_local = weight.shape
    targets = lax.axis_size("dec") // 2 - 1
    span = frames + ROW_TILE
    return pl.pallas_call(
        functools.partial(own_kernel, seq_len - span),
        out_shape=jax.ShapeDtypeStruct((targets, frames, width), BF16),
        in_specs=[HBM] + [VMEM] * 2,
        out_specs=VMEM,
        scratch_shapes=[pltpu.SMEM(routes.shape, jnp.int32)]
        + [pltpu.VMEM((width // PIECES // LANES, targets * span, LANES), F32)] * PIECES
        + [pltpu.SemaphoreType.DMA],
        compiler_params=pltpu.CompilerParams(vmem_limit_bytes=OWN_VMEM << 20),
        cost_estimate=matmul_cost(1, 1, 1),
        name="adapter_own",
    )(routes, slabs, weight)


def home_kernel(last_start, routes, slabs, weight, other, own, meta, product, meta_sem):
    route_copy = pltpu.make_async_copy(routes, meta, meta_sem)
    route_copy.start()
    multiply(slabs, weight, product)
    route_copy.wait()
    picks = [picks_of(meta, flip, [0], last_start)[0] for flip in (1, 0)]
    cut_rows(product, [other, own], picks, 0)


def adapter_home(frames, seq_len, routes, slabs, weight):
    width = weight.shape[0]
    span = frames + ROW_TILE
    return pl.pallas_call(
        functools.partial(home_kernel, seq_len - span),
        out_shape=[jax.ShapeDtypeStruct((frames, width), BF16)] * 2,
        in_specs=[HBM] + [VMEM] * 2,
        out_specs=[VMEM] * 2,
        scratch_shapes=[
            pltpu.SMEM(routes.shape, jnp.int32),
            pltpu.VMEM((width // LANES, 2 * span, LANES), F32),
            pltpu.SemaphoreType.DMA,
        ],
        compiler_params=pltpu.CompilerParams(vmem_limit_bytes=OWN_VMEM << 20),
        cost_estimate=matmul_cost(1, 1, 1),
        name="adapter_home",
    )(routes, slabs, weight)


def pair_sum_kernel(own, other, *outs):
    targets, frames, _ = own.shape
    size = frames // HALVES
    for at, out in enumerate(outs):
        half, step = divmod(at, targets)
        rows = pl.ds(half * size, size)
        out[...] = (own[step, rows, :].astype(F32) + other[step, rows, :].astype(F32)).astype(BF16)


def pair_sum(own, other):
    targets, frames, width = own.shape
    outs = pl.pallas_call(
        pair_sum_kernel,
        out_shape=[jax.ShapeDtypeStruct((frames // HALVES, width), BF16)] * (targets * HALVES),
        in_specs=[VMEM] * 2,
        out_specs=[VMEM] * (targets * HALVES),
        compiler_params=pltpu.CompilerParams(vmem_limit_bytes=24 << 20),
        name="pair_sum",
    )(own, other)
    return [outs[half * targets : (half + 1) * targets] for half in range(HALVES)]


def plane_sum_kernel(*refs):
    blocks, out = refs[:-1], refs[-1]
    total = blocks[0][...].astype(F32)
    for block in blocks[1:]:
        total = total + block[...].astype(F32)
    out[...] = total


def plane_sum(blocks):
    return pl.pallas_call(
        plane_sum_kernel,
        out_shape=jax.ShapeDtypeStruct(blocks[0].shape, F32),
        in_specs=[VMEM] * len(blocks),
        out_specs=VMEM,
        compiler_params=pltpu.CompilerParams(vmem_limit_bytes=24 << 20),
        name="plane_sum",
    )(*blocks)


def square_sum_kernel(own, other, along_x, along_y, keep_x, keep_y):
    size = keep_x.shape[0]
    first, second = pl.ds(0, size), pl.ds(size, size)

    def both(place, rows):
        return (own[place, rows, :].astype(F32) + other[place, rows, :].astype(F32)).astype(BF16)

    along_x[0, :, :] = both(0, first)
    along_x[1, :, :] = both(2, first)
    along_y[0, :, :] = both(1, second)
    along_y[1, :, :] = both(2, second)
    keep_x[...] = both(1, first)
    keep_y[...] = both(0, second)


def square_sum(own, other):
    _, frames, width = own.shape
    pair = jax.ShapeDtypeStruct((2, frames // 2, width), BF16)
    single = jax.ShapeDtypeStruct((frames // 2, width), BF16)
    return pl.pallas_call(
        square_sum_kernel,
        out_shape=[pair, pair, single, single],
        in_specs=[VMEM] * 2,
        out_specs=[VMEM] * 4,
        compiler_params=pltpu.CompilerParams(vmem_limit_bytes=24 << 20),
        name="pair_sum",
    )(own, other)


def relay_kernel(keep, arrived, out):
    out[...] = (keep[...].astype(F32) + arrived[1].astype(F32)).astype(BF16)


def relay(keep, arrived):
    return pl.pallas_call(
        relay_kernel,
        out_shape=jax.ShapeDtypeStruct(keep.shape, BF16),
        in_specs=[VMEM] * 2,
        out_specs=VMEM,
        compiler_params=pltpu.CompilerParams(vmem_limit_bytes=24 << 20),
        name="relay",
    )(keep, arrived)


def square_total_kernel(from_x, relayed_x, from_y, relayed_y, out):
    size = relayed_x.shape[0]
    out[:size, :] = from_x[0].astype(F32) + relayed_x[...].astype(F32)
    out[size:, :] = from_y[0].astype(F32) + relayed_y[...].astype(F32)


def square_total(from_x, relayed_x, from_y, relayed_y):
    size, width = relayed_x.shape
    return pl.pallas_call(
        square_total_kernel,
        out_shape=jax.ShapeDtypeStruct((2 * size, width), F32),
        in_specs=[VMEM] * 4,
        out_specs=VMEM,
        compiler_params=pltpu.CompilerParams(vmem_limit_bytes=24 << 20),
        name="plane_sum",
    )(from_x, relayed_x, from_y, relayed_y)


def swish_kernel(parts, first, valid, project, *refs):
    homes, blocks, outs, stream = refs[:2], refs[2:parts], refs[parts:-1], refs[-1]
    groups = len(outs) // 2
    frames, width = stream.shape
    c_local = outs[0].shape[1]
    total = sum(home[first : first + frames, :].astype(F32) for home in homes)
    for block in blocks:
        total = total + block[...].astype(F32)
    rows = first + lax.broadcasted_iota(jnp.int32, (frames, width), 0)
    stream[...] = jnp.where(rows < valid[0], total, 0.0).astype(BF16)
    for step in range(groups):
        at = pl.ds(pl.multiple_of(partner(step, groups) * c_local, c_local), c_local)
        outs[step][...] = dot(stream[...], project[step], NN).astype(outs[step].dtype)
        outs[groups + step][...] = stream[:, at].astype(outs[groups + step].dtype)


def swish(first, valid, project, homes, blocks):
    frames, width = blocks[0].shape
    blocks = homes + blocks
    groups, _, c_local = project.shape
    outs = pl.pallas_call(
        functools.partial(swish_kernel, len(blocks), first),
        out_shape=[jax.ShapeDtypeStruct((frames, c_local), F32 if step == 0 else BF16) for step in range(groups)] * 2,
        in_specs=[SMEM, VMEM] + [VMEM] * len(blocks),
        out_specs=[VMEM] * (2 * groups),
        scratch_shapes=[pltpu.VMEM((frames, width), BF16)],
        compiler_params=pltpu.CompilerParams(vmem_limit_bytes=24 << 20),
        cost_estimate=matmul_cost(frames, width, width),
        name="stream_and_swish",
    )(valid, project, *blocks)
    return outs[:groups], outs[groups:]


def spread_rows(padded, rows):
    frames, c_local = rows.shape
    edge = (padded.shape[0] - frames) // 2
    padded[:edge, :] = jnp.zeros((edge, c_local), F32)
    padded[edge + frames :, :] = jnp.zeros((edge, c_local), F32)
    padded[pl.ds(edge, frames), :] = rows


def edge_of(taps):
    return -(-((taps - 1) // 2) // 8) * 8


def transpose_kernel(expand, project, expand_t, project_t):
    groups, _, c_local = project_t.shape
    for step in range(groups):
        at = pl.ds(pl.multiple_of(partner(step, groups) * c_local, c_local), c_local)
        project_t[step, :, :] = project[at, :].T
        expand_t[step, :, :] = expand[at, :].T


def transposed(groups, expand, project):
    width, span = expand.shape
    c_local = width // groups
    return pl.pallas_call(
        transpose_kernel,
        out_shape=[
            jax.ShapeDtypeStruct((groups, span, c_local), BF16),
            jax.ShapeDtypeStruct((groups, width, c_local), BF16),
        ],
        in_specs=[VMEM] * 2,
        out_specs=[VMEM] * 2,
        compiler_params=pltpu.CompilerParams(vmem_limit_bytes=24 << 20),
        cost_estimate=matmul_cost(1, 1, 1),
        name="transposed_weights",
    )(expand, project)


def forward_kernel(valid, expand, taps_ref, scale, shift, inputs, value_out, gate_out, slope_out, padded):
    frames, c_local = value_out.shape
    taps = taps_ref.shape[0]
    half = (taps - 1) // 2
    edge = (padded.shape[0] - frames) // 2
    expanded = jnp.zeros((frames, 2 * c_local), F32)
    masks = [0]
    while len(masks) * frames < inputs.shape[0]:
        far = inputs.shape[0] // frames // 2 // len(masks)
        masks += [mask ^ far for mask in masks]
    for place, mask in enumerate(masks):
        at = pl.ds(pl.multiple_of((lax.axis_index("ch") ^ mask) * c_local, c_local), c_local)
        expanded = expanded + dot(inputs[place * frames : (place + 1) * frames, :], expand[at, :], NN)
    value = expanded[:, :c_local]
    gate = jax.nn.sigmoid(expanded[:, c_local:])
    rows = lax.broadcasted_iota(jnp.int32, (frames, c_local), 0)
    spread_rows(padded, jnp.where(rows < valid[0], value * gate, 0.0))
    depth = jnp.zeros((frames, c_local), F32)
    for tap in range(taps):
        depth = depth + taps_ref[tap : tap + 1, :] * padded[pl.ds(edge - half + tap, frames), :]
    shifted = depth * scale[...] + shift[...]
    sig = jax.nn.sigmoid(shifted)
    value_out[...] = value
    gate_out[...] = gate
    slope_out[...] = sig * (1.0 + shifted * (1.0 - sig)) * scale[...]


def forward(frames, valid, expand, taps, scale, shift, inputs):
    width, c_local = expand.shape[0], inputs.shape[1]
    return pl.pallas_call(
        forward_kernel,
        out_shape=[jax.ShapeDtypeStruct((frames, c_local), F32)] * 3,
        in_specs=[SMEM] + [VMEM] * 5,
        out_specs=[VMEM] * 3,
        scratch_shapes=[pltpu.VMEM((frames + 2 * edge_of(taps.shape[0]), c_local), F32)],
        compiler_params=pltpu.CompilerParams(vmem_limit_bytes=24 << 20),
        cost_estimate=matmul_cost(frames, width, 2 * c_local),
        name="forward_gates",
    )(valid, expand, taps, scale, shift, inputs)


def backward_kernel(parts, valid, expand_t, taps_ref, value_ref, gate_ref, slope, *refs):
    blocks, outs, padded = refs[:parts], refs[parts:-1], refs[-1]
    frames, c_local = value_ref.shape
    taps = taps_ref.shape[0]
    half = (taps - 1) // 2
    edge = (padded.shape[0] - frames) // 2
    total = blocks[0][...].astype(F32)
    for block in blocks[1:]:
        total = total + block[...].astype(F32)
    spread_rows(padded, total * slope[...])
    grad = jnp.zeros((frames, c_local), F32)
    for tap in range(taps):
        grad = grad + taps_ref[tap : tap + 1, :] * padded[pl.ds(edge + half - tap, frames), :]
    rows = lax.broadcasted_iota(jnp.int32, (frames, c_local), 0)
    grad = jnp.where(rows < valid[0], grad, 0.0)
    gate = gate_ref[...]
    grad_value = grad * gate
    grad_gate = grad_value * value_ref[...] * (1.0 - gate)
    grad_expanded = jnp.concatenate([grad_value.astype(BF16), grad_gate.astype(BF16)], axis=1)
    for step, out in enumerate(outs):
        out[...] = dot(grad_expanded, expand_t[step], NN).astype(out.dtype)


def backward(valid, expand_t, taps, value, gate, slope, blocks):
    frames, c_local = value.shape
    groups = expand_t.shape[0]
    return pl.pallas_call(
        functools.partial(backward_kernel, groups),
        out_shape=[jax.ShapeDtypeStruct((frames, c_local), F32 if step == 0 else BF16) for step in range(groups)],
        in_specs=[SMEM] + [VMEM] * (5 + groups),
        out_specs=[VMEM] * groups,
        scratch_shapes=[pltpu.VMEM((frames + 2 * edge_of(taps.shape[0]), c_local), F32)],
        compiler_params=pltpu.CompilerParams(vmem_limit_bytes=16 << 20),
        cost_estimate=matmul_cost(frames, 2 * c_local, c_local * groups),
        name="backward_module",
    )(valid, expand_t, taps, value, gate, slope, *blocks)


def partner(step, groups):
    return lax.rem(lax.axis_index("ch") + step, groups)


def swap(block, axis, count, mask):
    return lax.ppermute(block, axis, [(i, i ^ mask) for i in range(count)])


def turns(count):
    return sorted(range(1, count), key=lambda step: abs(2 * step - count))


def turn(block, count, step):
    return lax.ppermute(block, "ch", [(i, (i + step) % count) for i in range(count)])


def z_exchange(blocks):
    count = len(blocks)
    return [blocks[0]] + [turn(blocks[step], count, step) for step in turns(count)]


def z_gather(block, count):
    held, mask = block, count // 2
    while mask:
        arrived = swap(held, "ch", count, mask)
        held = jnp.concatenate([held, arrived], axis=0)
        mask //= 2
    return held


def summed(blocks):
    return sum(block.astype(F32) for block in blocks).astype(BF16)


def plane_exchange(blocks, count):
    return [swap(block, "dec", count, 2 * step) for step, block in enumerate(blocks, 1)]


def body(
    n_dec,
    n_ch,
    frame_cotangent,
    rollout_utterance,
    frame_offset,
    utterance_frames,
    normed_input,
    expand_weight,
    depth_kernel,
    norm_scale,
    norm_shift,
    project_weight,
    adapter_weight,
):
    u_local, frames, c_local = normed_input.shape
    width = expand_weight.shape[0]
    chips = n_dec // 2
    expand = expand_weight.reshape(width, 2 * c_local)
    taps = depth_kernel.astype(F32)
    scale, shift = norm_scale.reshape(1, c_local), norm_shift.reshape(1, c_local)

    seq_len = frame_cotangent.shape[1]
    routes = jnp.stack([rollout_utterance, frame_offset])
    for_other, own_slabs, home_slabs, weight = adapter_other(frames, routes, frame_cotangent, adapter_weight)
    from_other = swap(for_other, "dec", n_dec, 1)
    own = adapter_own(frames, seq_len, routes, own_slabs, weight)
    square = chips == 4
    sums = square_sum(own, from_other) if square else pair_sum(own, from_other)[0]
    sums, routes, own_input = lax.optimization_barrier((sums, routes, normed_input.reshape(frames, c_local)))
    if square:
        from_x, from_y = swap(sums[0], "dec", n_dec, 2), swap(sums[1], "dec", n_dec, 4)
        relayed_x = swap(relay(sums[2], from_x), "dec", n_dec, 4)
        relayed_y = swap(relay(sums[3], from_y), "dec", n_dec, 2)
        arrived = square_total(from_x, relayed_x, from_y, relayed_y)
    else:
        arrived = plane_sum(plane_exchange(sums, n_dec))
    home_other, home_own = adapter_home(frames, seq_len, routes, home_slabs, weight)
    homes = [home_own, swap(home_other, "dec", n_dec, 1)]
    inputs = z_gather(own_input, n_ch)
    expand_t, project_t = transposed(n_ch, expand, project_weight)
    value, gate, slope = forward(frames, utterance_frames, expand, taps, scale, shift, inputs)
    swish_parts, stream_parts = swish(0, utterance_frames, project_t, homes, [arrived])
    swish_parts = z_exchange(swish_parts)
    *early, late = turns(n_ch)
    stream_arrived = [stream_parts[0]] + [turn(stream_parts[step], n_ch, step) for step in early]
    parts = backward(utterance_frames, expand_t, taps, value, gate, slope, swish_parts)
    parts, late_part = lax.optimization_barrier((parts, stream_parts[late]))
    parts = z_exchange(parts)
    stream_parts = stream_arrived + [turn(late_part, n_ch, late)]
    return summed(stream_parts)[None], summed(parts)[None]


def solution(mesh):
    return jax.shard_map(
        functools.partial(body, mesh.shape["dec"], mesh.shape["ch"]),
        mesh=mesh,
        in_specs=(
            P("dec", None, "ch"),
            P("dec"),
            P("dec"),
            P("dec"),
            P("dec", None, "ch"),
            P(None, None, "ch"),
            P(None, "ch"),
            P("ch"),
            P("ch"),
            P(),
            P(None, "ch"),
        ),
        out_specs=(P("dec", None, "ch"), P("dec", None, "ch")),
        check_vma=False,
    )
```
